32 devices in a mesh: rows: 4 (over z), hid: 4 (over x, core), wid: 2 (over y).
Axes of the slice: x: 2, y: 2, z: 4, core: 2. Of those that a mesh axis runs over, the one named last changes fastest.
Arguments:
- inputs: bfloat16 [2, 8, 512, 1536], P(None, 'rows', 'hid', 'wid'), may hold values from -6 to 6
- starts: int32 [2, 8, 4], P(None, 'rows'), may hold values from 0 to 511, as said below
- norm_one: float32 [1536], P('wid'), may hold values from 0.5 to 1.5
- w_query: bfloat16 [1536, 1536], P('wid', 'hid'), may hold values from -0.15625 to 0.15625
- w_key: bfloat16 [1536, 1536], P('wid', 'hid'), may hold values from -0.15625 to 0.15625
- w_value: bfloat16 [1536, 1536], P('wid', 'hid'), may hold values from -0.15625 to 0.15625
- w_house: bfloat16 [1536, 1536], P('wid', 'hid'), may hold values from -0.15625 to 0.15625
- strength_weight: bfloat16 [1536, 12], P('wid', 'hid'), may hold values from -0.15625 to 0.15625
- b_beta: float32 [12], P('hid'), may hold values from -3 to 3
- w_out: bfloat16 [1536, 1536], P('hid', 'wid'), may hold values from -0.625 to 0.625
- norm_two: float32 [1536], P('wid'), may hold values from 0.5 to 1.5
- gate_weight: bfloat16 [1536, 4096], P('wid', 'hid'), may hold values from -0.15625 to 0.15625
- up_weight: bfloat16 [1536, 4096], P('wid', 'hid'), may hold values from -0.15625 to 0.15625
- w_down: bfloat16 [4096, 1536], P('hid', 'wid'), may hold values from -0.09375 to 0.09375
- cotangent: bfloat16 [2, 8, 512, 1536], P(None, 'rows', 'hid', 'wid'), may hold values from -6 to 6
Outputs:
- output: bfloat16 [2, 8, 512, 1536], P(None, 'rows', 'hid', 'wid')
- grad_input: float32 [2, 8, 512, 1536], P(None, 'rows', 'hid', 'wid')
- grad_norm_one: float32 [1536], P('wid')
- grad_query: float32 [1536, 1536], P('wid', 'hid')
- grad_key: float32 [1536, 1536], P('wid', 'hid')
- grad_value: float32 [1536, 1536], P('wid', 'hid')
- grad_house: float32 [1536, 1536], P('wid', 'hid')
- grad_beta_weight: float32 [1536, 12], P('wid', 'hid')
- grad_beta_bias: float32 [12], P('hid')
- grad_out: float32 [1536, 1536], P('hid', 'wid')
- grad_norm_two: float32 [1536], P('wid')
- grad_gate: float32 [1536, 4096], P('wid', 'hid')
- grad_up: float32 [1536, 4096], P('wid', 'hid')
- grad_down: float32 [4096, 1536], P('hid', 'wid')
The draws below stay inside these ranges and needn't reach their ends.
Inputs may be any that keep to these rules, and one draw needn't show every extreme that they name: In each packed row the 4 starts rise strictly and the first is 0.
All inputs are finite; a program needn't handle non-finite values.
Results may differ from the reference program's by a relative error of at most 0.02.
Values may be sent and summed in bfloat16 or wider, within the bound.
No kernel may reach another device: no remote copies, remote signals or barrier semaphores. Data moves between devices by JAX's collectives and lax.ppermute only.
A program may use at most 256 MiB of HBM per device.

```python
import jax
import jax.numpy as jnp
from jax import lax

D = 1536
HEADS = 12
FF = 4096
SEQ = 512
MICRO = 2
NDOC = 4
HD = 1536
ALLROWS = 8


def draw_starts(key, part):
    key = jax.random.fold_in(key, 7)
    keys = jax.random.split(key, MICRO * ALLROWS)

    def one_row(row_key):
        picked = jax.random.permutation(row_key, SEQ - 1)[:NDOC - 1] + 1
        return jnp.concatenate([jnp.zeros((1,), jnp.int32), jnp.sort(picked.astype(jnp.int32))])
    return jax.vmap(one_row)(keys).reshape(MICRO, ALLROWS, NDOC)


def shard_levels(key, shape, pieces, smallest, top_value):
    def one(position, blocks):
        steps = jax.random.uniform(jax.random.fold_in(jax.random.fold_in(key, 6), position), (blocks,), jnp.float32, smallest / len(pieces), top_value / len(pieces))
        return jnp.repeat(jnp.exp(steps), shape[position] // blocks).reshape((-1,) + (1,) * (len(shape) - position - 1))

    loudness = one(*pieces[0])
    for cut in pieces[1:]:
        loudness = loudness * one(*cut)
    return loudness


def scatter_about(stream_key, extent, deviation, limit, cuts=(), kind=jnp.bfloat16):
    loudness = shard_levels(stream_key, extent, cuts, -0.22, 0.18) if cuts else 1.0
    drawn = jax.random.normal(stream_key, extent, jnp.float32) * deviation * loudness
    return jnp.minimum(jnp.maximum(drawn, -limit), limit).astype(kind)


def setup_inputs(seed: int = 0) -> dict:
    key_list = jax.random.split(jax.random.key(seed), 16)
    return {
        "inputs": scatter_about(key_list[0], (MICRO, ALLROWS, SEQ, D), 1.0, 6.0, ((1, 4), (2, 4), (3, 2))),
        "starts": draw_starts(jax.random.fold_in(key_list[15], 71), 0),
        "norm_one": jnp.clip(1.0 + 0.1 * jax.random.normal(key_list[2], (D,), jnp.float32), 0.5, 1.5),
        "w_query": scatter_about(key_list[3], (D, HD), D ** -0.5, 0.15625, ((0, 2), (1, 4))),
        "w_key": scatter_about(key_list[4], (D, HD), D ** -0.5, 0.15625, ((0, 2), (1, 4))),
        "w_value": scatter_about(key_list[5], (D, HD), D ** -0.5, 0.15625, ((0, 2), (1, 4))),
        "w_house": scatter_about(key_list[6], (D, HD), D ** -0.5, 0.15625, ((0, 2), (1, 4))),
        "strength_weight": scatter_about(key_list[7], (D, HEADS), D ** -0.5, 0.15625, ((0, 2), (1, 4))),
        "b_beta": scatter_about(key_list[8], (HEADS,), 1.0, 3.0, ((0, 4),), jnp.float32),
        "w_out": scatter_about(key_list[9], (HD, D), (HD // 16) ** -0.5, 0.625, ((0, 4), (1, 2))),
        "norm_two": jnp.clip(1.0 + 0.1 * jax.random.normal(key_list[10], (D,), jnp.float32), 0.5, 1.5),
        "gate_weight": scatter_about(key_list[11], (D, FF), D ** -0.5, 0.15625, ((0, 2), (1, 4))),
        "up_weight": scatter_about(key_list[12], (D, FF), D ** -0.5, 0.15625, ((0, 2), (1, 4))),
        "w_down": scatter_about(key_list[13], (FF, D), FF ** -0.5, 0.09375, ((0, 4), (1, 2))),
        "cotangent": scatter_about(key_list[14], (MICRO, ALLROWS, SEQ, D), 1.0, 6.0, ((1, 4), (2, 4), (3, 2))),
    }


EPS = 1e-06

@jax.custom_vjp
def low(v):
    return lax.optimization_barrier(v.astype(jnp.bfloat16)).astype(jnp.float32)

@jax.custom_vjp
def low_back(v):
    return v

def low_keep(v):
    return (low(v), None)

def low_pass(kept, grad):
    return (grad,)

def back_keep(v):
    return (v, None)

def back_low(kept, grad):
    return (low(grad),)
low.defvjp(low_keep, low_pass)
low_back.defvjp(back_keep, back_low)

def households(query, keys, values, house, braw, row_starts):
    length = query.shape[0]
    heads = braw.shape[1]
    high = lax.Precision.HIGHEST

    def split(arr):
        return arr.reshape(length, heads, -1).transpose(1, 0, 2)
    qh, kh, vh, uh = (split(query), split(keys), split(values), split(house))
    wdir = uh * lax.rsqrt(lax.optimization_barrier(jnp.sum(uh * uh, -1, keepdims=True)) + EPS)
    beta = 2.0 * jax.nn.sigmoid(braw).T
    place = jnp.arange(length)
    docs = lax.optimization_barrier(jnp.sum((place[:, None] >= row_starts[None, :]).astype(jnp.int32), 1))
    below = place[:, None] > place[None, :]
    upto = place[:, None] >= place[None, :]
    allowed = upto & (docs[:, None] == docs[None, :])
    mixing = jnp.einsum('hid,hjd->hij', wdir, wdir, precision=high)
    system = jnp.eye(length, dtype=query.dtype) + jnp.where(below, mixing, 0.0) * beta[:, None, :]
    right = jnp.where(below, jnp.einsum('hid,hjd->hij', wdir, kh, precision=high), 0.0)
    coeff = jax.scipy.linalg.solve_triangular(system, right, lower=True, unit_diagonal=True)
    direct = jnp.where(upto, jnp.einsum('hid,hjd->hij', qh, kh, precision=high), 0.0)
    cross = jnp.where(upto, jnp.einsum('hid,hjd->hij', qh, wdir, precision=high), 0.0) * beta[:, None, :]
    scores = (direct - jnp.einsum('hit,htj->hij', cross, coeff, precision=high)) / jnp.sqrt(float(qh.shape[-1]))
    scores = jnp.where(allowed, scores, -1e+30)
    top = lax.optimization_barrier(jnp.max(scores, -1, keepdims=True))
    weights = jnp.exp(scores - top)
    weights = weights / lax.optimization_barrier(jnp.sum(weights, -1, keepdims=True))
    result = jnp.einsum('hij,hjd->hid', weights, vh, precision=high)
    return result.transpose(1, 0, 2).reshape(length, -1)

def block(xs, row_starts, params):
    g_one, wq, wk, wv, wu, wb, bb, wo, g_two, wg, wup, wd = params
    high = lax.Precision.HIGHEST

    def mult(a, b):
        return jnp.dot(a, b, precision=high)
    scale_one = lax.rsqrt(lax.optimization_barrier(jnp.mean(xs * xs, -1, keepdims=True)) + EPS)
    normed = low(xs * scale_one * g_one)
    query = low_back(mult(normed, wq))
    keys = low_back(mult(normed, wk))
    values = low_back(mult(normed, wv))
    house = low_back(mult(normed, wu))
    braw = low_back(mult(normed, wb) + bb)
    attn = low(households(query, keys, values, house, braw, row_starts))
    branch = low_back(mult(attn, wo))
    middle = xs + branch
    scale_two = lax.rsqrt(lax.optimization_barrier(jnp.mean(middle * middle, -1, keepdims=True)) + EPS)
    normed_two = low(middle * scale_two * g_two)
    gate = low_back(mult(normed_two, wg))
    upper = low_back(mult(normed_two, wup))
    act = low(jax.nn.silu(gate) * upper)
    return middle + mult(act, wd)

def reference(inputs, starts, norm_one, w_query, w_key, w_value, w_house, strength_weight, b_beta, w_out, norm_two, gate_weight, up_weight, w_down, cotangent):
    params = tuple((a.astype(jnp.float32) for a in (norm_one, w_query, w_key, w_value, w_house, strength_weight, b_beta, w_out, norm_two, gate_weight, up_weight, w_down)))
    flat = inputs.astype(jnp.float32).reshape(MICRO * ALLROWS, SEQ, D)
    flat_starts = starts.reshape(MICRO * ALLROWS, NDOC)

    def forward(xs, weights):
        step = jax.checkpoint(lambda pair: block(pair[0], pair[1], weights))
        return lax.map(step, (xs, flat_starts))
    result, pull = jax.vjp(forward, flat, params)
    grad_x, grads = pull(cotangent.astype(jnp.float32).reshape(flat.shape))
    shape = inputs.shape
    return (result.reshape(shape).astype(jnp.bfloat16), grad_x.reshape(shape), grads[0], grads[1], grads[2], grads[3], grads[4], grads[5], grads[6], grads[7], grads[8], grads[9], grads[10], grads[11])
```

```python
import jax
import jax.numpy as jnp
from jax import lax
from jax.experimental import pallas as pl
from jax.experimental.pallas import tpu as pltpu
from jax.sharding import PartitionSpec as P

EPS = 1e-06
F32 = jnp.float32
BF = jnp.bfloat16


def mul(a, b):
    return lax.dot_general(a, b, (((1,), (0,)), ((), ())), preferred_element_type=F32)


def mul_t(a, b):
    return lax.dot_general(a, b, (((1,), (1,)), ((), ())), preferred_element_type=F32)


def parts_of(a):
    high = a.astype(BF)
    return high, (a - high.astype(F32)).astype(BF)


def mul_fine(a, b):
    ah, al = parts_of(a)
    bh, bl = parts_of(b)
    return mul(jnp.concatenate([ah, al], 1), jnp.concatenate([bh, bh], 0)) + mul(ah, bl)


def grid_of(rows, cols, row0, col0):
    return (
        lax.broadcasted_iota(jnp.int32, (rows, cols), 0) + row0,
        lax.broadcasted_iota(jnp.int32, (rows, cols), 1) + col0,
    )


def first_of(place, starts_ref):
    begin = jnp.zeros_like(place)
    for n in range(starts_ref.shape[0]):
        begin = jnp.where(place >= starts_ref[n], starts_ref[n], begin)
    return begin


def directions(u, braw):
    scale = lax.rsqrt(jnp.sum(u * u, -1, keepdims=True) + EPS)
    wdir = u * scale
    beta = 2.0 * jax.nn.sigmoid(braw)
    return scale, wdir, beta


def unit_inverses(tiles):
    size = tiles[0].shape[0]
    row, col = grid_of(size, size, 0, 0)
    eye = jnp.where(row == col, 1.0, 0.0)
    near = (row // 8) == (col // 8)
    base = [jnp.where(near, n, 0.0) for n in tiles]
    two = [mul_fine(n, n) for n in base]
    three = [mul_fine(n, m) for n, m in zip(base, two)]
    four = [mul_fine(m, m) for m in two]
    low = [eye + a + b + c for a, b, c in zip(base, two, three)]
    done = [p + mul_fine(p, f) for p, f in zip(low, four)]
    span = 8
    while span < size:
        cross = ((row // (2 * span)) == (col // (2 * span))) & ((row // span) != (col // span))
        part = [mul_fine(jnp.where(cross, n, 0.0), d) for n, d in zip(tiles, done)]
        done = [d + mul_fine(d, p) for d, p in zip(done, part)]
        span *= 2
    return done


def forward_kernel(starts_ref, q_ref, k_ref, v_ref, u_ref, b_ref, o_ref, p_ref, c_ref, t_ref):
    length = q_ref.shape[0]
    heads = b_ref.shape[1]
    dim = q_ref.shape[1] // heads
    half, tile = length // 2, length // 4
    soft = dim ** -0.5
    row, col = grid_of(length, half, 0, 0)
    row1, col1 = grid_of(half, half, half, half)
    begin = first_of(lax.broadcasted_iota(jnp.int32, (length, 1), 0), starts_ref)
    from_doc = col >= begin
    strict_a = from_doc & (col < row)
    upto_a = from_doc & (col <= row)
    strict_b = (col1 >= begin[half:]) & (col1 < row1)
    upto_b = (col1 >= begin[half:]) & (col1 <= row1)

    state = []
    tiles = []
    for h in range(heads):
        at = slice(h * dim, (h + 1) * dim)
        _, wdir, beta = directions(u_ref[:, at], b_ref[:, h : h + 1])
        wd, wb = wdir.astype(BF), (wdir * beta).astype(BF)
        la = jnp.where(strict_a, mul_t(wd, wb[:half]), 0.0)
        lb = jnp.where(strict_b, mul_t(wd[half:], wb[half:]), 0.0)
        state.append((wd, wb, la, lb))
        tiles += [-la[:tile, :tile], -la[tile:half, tile:], -lb[:tile, :tile], -lb[tile:, tile:]]
    done = unit_inverses(tiles)
    for h in range(heads):
        at = slice(h * dim, (h + 1) * dim)
        wd, wb, la, lb = state[h]
        whole = []
        for n, lower in enumerate((la[:half], lb)):
            d0, d1 = done[4 * h + 2 * n], done[4 * h + 2 * n + 1]
            d10 = -mul_fine(d1, mul_fine(lower[tile:, :tile], d0))
            t = jnp.concatenate(
                [jnp.concatenate([d0, jnp.zeros_like(d0)], 1), jnp.concatenate([d10, d1], 1)], 0
            )
            t_ref[h, n] = t.T.astype(BF)
            whole.append(t.astype(BF))
        k = k_ref[:, at]
        q = q_ref[:, at]
        ra = jnp.where(strict_a, mul_t(wd, k[:half]), 0.0)
        rb = jnp.where(strict_b, mul_t(wd[half:], k[half:]), 0.0)
        c00 = mul(whole[0], ra[:half].astype(BF)).astype(BF)
        g10 = ra[half:] - mul(la[half:].astype(BF), c00)
        c1 = mul(whole[1], jnp.concatenate([g10, rb], 1).astype(BF)).astype(BF)
        c_ref[h, :half, :half] = c00
        c_ref[h, half:, :] = c1
        xa = jnp.where(upto_a, mul_t(q, wb[:half]), 0.0).astype(BF)
        xb = jnp.where(upto_b, mul_t(q[half:], wb[half:]), 0.0).astype(BF)
        sa = mul_t(q, k[:half]) - mul(xa, c00)
        s0 = jnp.where(upto_a[:half], sa[:half], -1e30)
        low = mul(xb, c1)
        s10 = jnp.where(from_doc[half:], sa[half:] - low[:, :half], -1e30)
        s11 = jnp.where(upto_b, mul_t(q[half:], k[half:]) - low[:, half:], -1e30)
        top = jnp.max(s0, -1, keepdims=True)
        w = jnp.exp((s0 - top) * soft)
        w = (w * (1.0 / jnp.sum(w, -1, keepdims=True))).astype(BF)
        p_ref[h, :half, :half] = w
        v = v_ref[:, at]
        o_ref[:half, at] = mul(w, v[:half]).astype(BF)
        s1 = jnp.concatenate([s10, s11], 1)
        top = jnp.max(s1, -1, keepdims=True)
        w = jnp.exp((s1 - top) * soft)
        w = (w * (1.0 / jnp.sum(w, -1, keepdims=True))).astype(BF)
        p_ref[h, half:, :] = w
        o_ref[half:, at] = mul(w, v).astype(BF)


def backward_kernel(
    starts_ref, q_ref, k_ref, v_ref, u_ref, b_ref, do_ref, p_ref, c_ref, t_ref, dqv_ref, duk_ref, db_ref
):
    length = q_ref.shape[0]
    heads = b_ref.shape[1]
    dim = q_ref.shape[1] // heads
    half = length // 2
    soft = dim ** -0.5
    row, col = grid_of(length, half, 0, 0)
    row1, col1 = grid_of(half, half, half, half)
    begin = first_of(lax.broadcasted_iota(jnp.int32, (length, 1), 0), starts_ref)
    from_doc = col >= begin
    strict_a = from_doc & (col < row)
    upto_a = from_doc & (col <= row)
    strict_b = (col1 >= begin[half:]) & (col1 < row1)
    upto_b = (col1 >= begin[half:]) & (col1 <= row1)
    early, late = grid_of(half, length, 0, 0)
    begin_t = first_of(lax.broadcasted_iota(jnp.int32, (1, length), 1), starts_ref)
    from_doc_t = early >= begin_t
    upto_a_t = from_doc_t & (early <= late)
    early1, late1 = grid_of(half, half, half, half)
    upto_b_t = (early1 >= begin_t[:, half:]) & (early1 <= late1)
    for h in range(heads):
        at = slice(h * dim, (h + 1) * dim)
        scale, wdir, beta = directions(u_ref[:, at], b_ref[:, h : h + 1])
        wd, wb = wdir.astype(BF), (wdir * beta).astype(BF)
        q, k, v, do = q_ref[:, at], k_ref[:, at], v_ref[:, at], do_ref[:, at]
        qt, wdt, dot_ = q.T, wd.T, do.T
        p0, p1 = p_ref[h, :half, :half], p_ref[h, half:, :]
        c00, c1 = c_ref[h, :half, :half], c_ref[h, half:, :]
        t0, t1 = t_ref[h, 0], t_ref[h, 1]
        p0f, p1f = p0.astype(F32), p1.astype(F32)
        dp0 = mul_t(do[:half], v[:half])
        dp1 = mul_t(do[half:], v)
        ds0 = p0f * (dp0 - jnp.sum(p0f * dp0, -1, keepdims=True)) * soft
        ds1 = p1f * (dp1 - jnp.sum(p1f * dp1, -1, keepdims=True)) * soft
        ds0, ds1 = ds0.astype(BF), ds1.astype(BF)
        dsa = jnp.concatenate([ds0, ds1[:, :half]], 0)
        dxa = jnp.where(upto_a, mul_t(dsa, c00), 0.0).astype(BF)
        dxb = jnp.where(upto_b, mul_t(ds1, c1), 0.0).astype(BF)
        xta = jnp.where(upto_a_t, mul_t(wb[:half], q), 0.0).astype(BF)
        xtb = jnp.where(upto_b_t, mul_t(wb[half:], q[half:]), 0.0).astype(BF)
        lta = jnp.where(from_doc_t[:, half:], mul_t(wb[:half], wd[half:]), 0.0).astype(BF)
        dc00 = mul(xta, dsa)
        dc1 = mul(xtb, ds1).astype(BF)
        z1 = mul(t1, dc1)
        z10 = jnp.where(from_doc[half:], z1[:, :half], 0.0).astype(BF)
        z11 = jnp.where(strict_b, z1[:, half:], 0.0).astype(BF)
        z00 = mul(t0, (dc00 - mul(lta, z10)).astype(BF))
        z00 = jnp.where(strict_a[:half], z00, 0.0).astype(BF)
        za = jnp.concatenate([z00, z10], 0)
        z1 = jnp.concatenate([z10, z11], 1)
        dla = jnp.where(strict_a, mul_t(za, c00), 0.0).astype(BF)
        dlb = jnp.where(strict_b, mul_t(z1, c1), 0.0).astype(BF)
        dq0 = mul(ds0, k[:half]) - mul(dxa[:half], wb[:half])
        dq1 = mul(ds1, k) - mul(dxa[half:], wb[:half]) - mul(dxb, wb[half:])
        dk0 = mul(qt, dsa) - mul(wdt, za)
        dk1 = mul(qt[:, half:], ds1[:, half:]) - mul(wdt[:, half:], z11)
        y0 = mul(wdt, dla) - mul(qt, dxa)
        y1 = mul(wdt[:, half:], dlb) - mul(qt[:, half:], dxb)
        dv0 = mul(dot_[:, :half], p0) + mul(dot_[:, half:], p1[:, :half])
        dv1 = mul(dot_[:, half:], p1[:, half:])
        dw0 = mul(dla[:half], wb[:half]) - mul(z00, k[:half])
        dw1 = mul(dla[half:], wb[:half]) + mul(dlb, wb[half:]) - mul(z1, k)
        y = jnp.concatenate([y0, y1], 1).T
        dwd = beta * y + jnp.concatenate([dw0, dw1], 0)
        dbeta = jnp.sum(wdir * y, -1, keepdims=True)
        du = scale * (dwd - wdir * jnp.sum(wdir * dwd, -1, keepdims=True))
        width = heads * dim
        then = slice(width + h * dim, width + (h + 1) * dim)
        dqv_ref[:half, at] = dq0.astype(BF)
        dqv_ref[half:, at] = dq1.astype(BF)
        dqv_ref[:, then] = jnp.concatenate([dv0, dv1], 1).T.astype(BF)
        duk_ref[:, at] = du.astype(BF)
        duk_ref[:, then] = jnp.concatenate([dk0, dk1], 1).T.astype(BF)
        db_ref[:, h : h + 1] = (dbeta * beta * (1.0 - 0.5 * beta)).astype(BF)


def attn_forward(starts, q, k, v, u, braw):
    length, heads = braw.shape
    half = length // 2
    vm = pl.BlockSpec(memory_space=pltpu.VMEM)
    return pl.pallas_call(
        forward_kernel,
        in_specs=[pl.BlockSpec(memory_space=pltpu.SMEM)] + [vm] * 5,
        out_specs=[vm] * 4,
        out_shape=[
            jax.ShapeDtypeStruct(q.shape, BF),
            jax.ShapeDtypeStruct((heads, length, length), BF),
            jax.ShapeDtypeStruct((heads, length, length), BF),
            jax.ShapeDtypeStruct((heads, 2, half, half), BF),
        ],
        compiler_params=pltpu.CompilerParams(vmem_limit_bytes=48 * 2**20),
        name="attn_forward",
    )(starts, q, k, v, u, braw)


def attn_backward(starts, q, k, v, u, braw, do, p, c, t):
    length, heads = braw.shape
    vm = pl.BlockSpec(memory_space=pltpu.VMEM)
    return pl.pallas_call(
        backward_kernel,
        in_specs=[pl.BlockSpec(memory_space=pltpu.SMEM)] + [vm] * 9,
        out_specs=[vm] * 3,
        out_shape=[
            jax.ShapeDtypeStruct((length, 2 * q.shape[1]), BF),
            jax.ShapeDtypeStruct((length, 2 * q.shape[1]), BF),
            jax.ShapeDtypeStruct((length, heads), BF),
        ],
        compiler_params=pltpu.CompilerParams(vmem_limit_bytes=48 * 2**20),
        name="attn_backward",
    )(starts, q, k, v, u, braw, do, p, c, t)


def dot_rows(a, b):
    return lax.dot_general(a, b, (((0,), (0,)), ((), ())), preferred_element_type=F32)


def swap_wid(a):
    return lax.ppermute(a, "wid", [(0, 1), (1, 0)])


def swap_core(a):
    return lax.ppermute(a, "hid", [(0, 1), (1, 0), (2, 3), (3, 2)])


def swap_chip(a):
    return lax.ppermute(a, "hid", [(0, 2), (2, 0), (1, 3), (3, 1)])


def sum_rows(parts):
    n = lax.axis_size("rows")
    if n != 4:
        return [lax.psum(p, "rows") for p in parts]
    place = lax.axis_index("rows")
    inner = (place == 1) | (place == 2)
    done = []
    for p in parts:
        got = lax.ppermute(p, "rows", [(0, 1), (3, 2)])
        side = (p.astype(F32) + got.astype(F32)).astype(BF)
        got = lax.ppermute(side, "rows", [(1, 2), (2, 1)])
        whole = (side.astype(F32) + got.astype(F32)).astype(BF)
        got = lax.ppermute(whole, "rows", [(1, 0), (2, 3)])
        done.append(jnp.where(inner, whole, got))
    return done


def pick(pair, first):
    a, b = pair
    return jnp.where(first, a, b), jnp.where(first, b, a)


def on_device(
    inputs,
    starts,
    norm_one,
    w_query,
    w_key,
    w_value,
    w_house,
    strength_weight,
    b_beta,
    w_out,
    norm_two,
    gate_weight,
    up_weight,
    w_down,
    cotangent,
):
    micros, _, block, part = inputs.shape
    width = 2 * part
    length = 4 * block
    heads_cols = w_query.shape[1]
    wid = lax.axis_index("wid")
    hid = lax.axis_index("hid")
    core, chip = hid % 2, hid // 2
    core0, chip0, wid0 = core == 0, chip == 0, wid == 0

    def take(a, axis, index):
        return lax.dynamic_index_in_dim(a, index, axis, keepdims=False)

    x_far = swap_wid(take(inputs, 1, 1 - wid))
    w_uk = jnp.concatenate([w_house, w_key], 1)
    w_qv = jnp.concatenate([w_query, w_value], 1)
    uk_far = swap_wid(w_uk)
    qv_far = swap_wid(w_qv)
    sw_far = swap_wid(strength_weight)
    gains = jnp.stack([norm_one, norm_two])
    gains = jnp.concatenate([gains, swap_wid(gains)], 1)
    out_far = swap_wid(w_out)
    gate_far = swap_wid(gate_weight)
    up_far = swap_wid(up_weight)
    down_far = swap_wid(w_down)
    g_far = swap_wid(take(cotangent, 1, 1 - wid))
    row_starts = take(starts, 1, wid)

    def gather_chip(mine, far):
        mine = jnp.concatenate([mine, far], -1)
        a, b = pick((mine, swap_chip(mine)), chip0)
        return jnp.stack([a, b], 1).reshape(micros, 2 * block, width)

    def natural(mine, peer):
        cols = mine.shape[-1]
        a, b = pick((mine.reshape(2, block, cols), peer.reshape(2, block, cols)), core0)
        return jnp.stack([a, b], 1).reshape(length, cols)

    def split_cores(a):
        cols = a.shape[-1]
        a = a.reshape(2, 2, block, cols)
        return (
            take(a, 1, core).reshape(2 * block, cols),
            take(a, 1, 1 - core).reshape(2 * block, cols),
        )

    def both(a, own, far):
        return jnp.concatenate([mul(a, own), mul(a, far)], 1)

    def both_t(a, own, far):
        return jnp.concatenate([mul_t(a, own), mul_t(a, far)], 1)

    def over(a, own, far):
        return mul(a[:, :part], own) + mul(a[:, part:], far)

    def over_t(a, own, far):
        return mul_t(a[:, :part], own) + mul_t(a[:, part:], far)

    def chip_sum(keep, send):
        got = swap_core(send.astype(BF))
        return keep + got.astype(F32)

    def full_sum(keep, send):
        low = chip_sum(keep, send).astype(BF)
        return low.astype(F32) + swap_chip(low).astype(F32)

    def block_sum(keep, send):
        low = chip_sum(keep, send).reshape(2, block, width)
        got = swap_chip(take(low, 0, 1 - chip).astype(BF))
        return take(low, 0, chip) + got.astype(F32)

    def my_block(a):
        return take(a.reshape(2, block, a.shape[-1]), 0, chip)

    x_half = gather_chip(take(inputs, 1, wid), x_far).astype(F32)
    scale_one = lax.rsqrt(jnp.mean(x_half * x_half, -1, keepdims=True) + EPS)
    nm_half = (x_half * scale_one * gains[0]).astype(BF)
    nm_peer = swap_core(nm_half)
    nm = jnp.concatenate([natural(nm_half[m], nm_peer[m]) for m in range(micros)], 0)
    g_half = gather_chip(take(cotangent, 1, wid), g_far)
    g_peer = swap_core(g_half)

    uk = over(nm, w_uk, uk_far)
    braw = over(nm, strength_weight, sw_far) + b_beta
    qv = over(nm, w_qv, qv_far)
    house, keys = uk[:, :heads_cols], uk[:, heads_cols:].astype(BF)
    query, values = qv[:, :heads_cols].astype(BF), qv[:, heads_cols:].astype(BF)

    saved = []
    attn_keep, attn_send = [], []
    n2_all, mids, scales, acts, dgs, dus, outs = [], [], [], [], [], [], []
    for m in range(micros):
        at = slice(m * length, (m + 1) * length)
        args = (row_starts[m], query[at], keys[at], values[at], house[at], braw[at])
        attn, p, c, t = attn_forward(*args)
        saved.append((args, p, c, t))
        keep, send = split_cores(attn)
        attn_keep.append(keep)
        attn_send.append(send)
        mid = x_half[m] + full_sum(both(keep, w_out, out_far), both(send, w_out, out_far))
        scale_two = lax.rsqrt(jnp.mean(mid * mid, -1, keepdims=True) + EPS)
        n2 = (mid * scale_two * gains[1]).astype(BF)
        n2 = jnp.concatenate([n2, swap_core(n2)], 0)
        n2_all.append(n2)
        mids.append(mid)
        scales.append(scale_two)
    g_all = jnp.concatenate(
        [a for m in range(micros) for a in (g_half[m], g_peer[m])], 0
    )
    for m in range(micros):
        gm = jnp.concatenate([g_half[m], g_peer[m]], 0)
        d_act = over_t(gm, w_down, down_far)
        gate = over(n2_all[m], gate_weight, gate_far)
        upper = over(n2_all[m], up_weight, up_far)
        sigma = jax.nn.sigmoid(gate)
        swish = gate * sigma
        act = (swish * upper).astype(BF)
        acts.append(act)
        dgs.append((d_act * upper * sigma * (1.0 + gate * (1.0 - sigma))).astype(BF))
        dus.append((d_act * swish).astype(BF))
    n2_all = jnp.concatenate(n2_all, 0)
    act_all = jnp.concatenate(acts, 0)
    dg_all = jnp.concatenate(dgs, 0)
    du_all = jnp.concatenate(dus, 0)

    def wid_sum(own, far):
        return (own + swap_wid(far.astype(BF)).astype(F32)).astype(BF)

    def grad_rows(a, b):
        return wid_sum(dot_rows(a[:, :part], b), dot_rows(a[:, part:], b))

    def grad_cols(a, b):
        return wid_sum(dot_rows(a, b[:, :part]), dot_rows(a, b[:, part:]))

    down_low = grad_cols(act_all, g_all)
    gate_low = grad_rows(n2_all, dg_all)
    up_low = grad_rows(n2_all, du_all)

    half = 2 * block
    d_mids, d_branches = [], []
    gain_two = 0.0
    for m in range(micros):
        dg, du = dgs[m], dus[m]

        def back(s):
            return both_t(dg[s], gate_weight, gate_far) + both_t(du[s], up_weight, up_far)

        dn = full_sum(back(slice(0, half)), back(slice(half, None)))
        mid, scale = mids[m], scales[m]
        gain_two = gain_two + 0.5 * jnp.sum(dn * mid * scale, 0)
        inner = jnp.mean(mid * gains[1] * dn, -1, keepdims=True)
        d_mid = g_half[m].astype(F32) + scale * gains[1] * dn - mid * scale * scale * scale * inner
        low = d_mid.astype(BF)
        d_branches.append(jnp.concatenate([low, swap_core(low)], 0))
        d_mids.append(d_mid)

    for m in range(micros):
        feed = block_sum(
            both(acts[m][:half], w_down, down_far), both(acts[m][half:], w_down, down_far)
        )
        outs.append((my_block(mids[m]) + feed).astype(BF))

    db_all = jnp.concatenate(d_branches, 0)
    attn_all = jnp.concatenate(
        [a for m in range(micros) for a in (attn_keep[m], attn_send[m])], 0
    )
    out_low = grad_cols(attn_all, db_all)

    dqvs, duks, dbs, dxs = [], [], [], []
    gain_one = 0.0
    for m in range(micros):
        args, p, c, t = saved[m]
        d_attn = over_t(d_branches[m], w_out, out_far).astype(BF)
        d_attn = natural(d_attn[:half], d_attn[half:])
        dqv, duk, db = attn_backward(*args, d_attn, p, c, t)
        dqvs.append(dqv)
        duks.append(duk)
        dbs.append(db)
        pairs = (split_cores(dqv), split_cores(duk), split_cores(db))

        def back_one(n):
            return (
                both_t(pairs[0][n], w_qv, qv_far)
                + both_t(pairs[1][n], w_uk, uk_far)
                + both_t(pairs[2][n], strength_weight, sw_far)
            )

        dn = block_sum(back_one(0), back_one(1))
        x = my_block(x_half[m])
        scale = my_block(scale_one[m])
        gain_one = gain_one + jnp.sum(dn * x * scale, 0)
        inner = jnp.mean(x * gains[0] * dn, -1, keepdims=True)
        dxs.append(
            my_block(d_mids[m]) + scale * gains[0] * dn - x * scale * scale * scale * inner
        )
    dqv_all = jnp.concatenate(dqvs, 0)
    duk_all = jnp.concatenate(duks, 0)
    db_all = jnp.concatenate(dbs, 0)
    qv_low = grad_rows(nm, dqv_all)
    uk_low = grad_rows(nm, duk_all)

    down_low, gate_low, up_low, out_low, qv_low, uk_low = sum_rows(
        [down_low, gate_low, up_low, out_low, qv_low, uk_low]
    )
    strength = dot_rows(nm, db_all)
    bias = jnp.sum(db_all.astype(F32), 0)
    small = jnp.stack([gain_one, gain_two])
    small = small[:, :part] + swap_wid(small[:, part:])
    strength = strength[:part] + swap_wid(strength[part:])
    bias = bias + swap_wid(bias)
    strength, bias = lax.psum((strength, bias), "rows")
    small = lax.psum(small, ("rows", "hid"))

    def rows_back(values, kind):
        own = jnp.stack([v[:, :part] for v in values])
        far = swap_wid(jnp.stack([v[:, part:].astype(BF) for v in values])).astype(kind)
        a, b = pick((own, far), wid0)
        return jnp.stack([a, b], 1)

    def f(a):
        return a.astype(F32)

    return (
        rows_back(outs, BF),
        rows_back(dxs, F32),
        small[0],
        f(qv_low[:, :heads_cols]),
        f(uk_low[:, heads_cols:]),
        f(qv_low[:, heads_cols:]),
        f(uk_low[:, :heads_cols]),
        strength,
        bias,
        f(out_low),
        small[1],
        f(gate_low),
        f(up_low),
        f(down_low),
    )


def solution(mesh):
    tokens = P(None, "rows", "hid", "wid")
    tall, flat = P("wid", "hid"), P("hid", "wid")
    return jax.shard_map(
        on_device,
        mesh=mesh,
        in_specs=(
            tokens,
            P(None, "rows", None),
            P("wid"),
            tall,
            tall,
            tall,
            tall,
            tall,
            P("hid"),
            flat,
            P("wid"),
            tall,
            tall,
            flat,
            tokens,
        ),
        out_specs=(
            tokens,
            tokens,
            P("wid"),
            tall,
            tall,
            tall,
            tall,
            tall,
            P("hid"),
            flat,
            P("wid"),
            tall,
            tall,
            flat,
        ),
        check_vma=False,
    )
```

```python
import jax
import jax.numpy as jnp
from jax import lax
from jax.experimental import pallas as pl
from jax.experimental.pallas import tpu as pltpu
from jax.sharding import PartitionSpec as P

EPS = 1e-06
F32 = jnp.float32
BF = jnp.bfloat16


def mul(a, b):
    return lax.dot_general(a, b, (((1,), (0,)), ((), ())), preferred_element_type=F32)


def mul_t(a, b):
    return lax.dot_general(a, b, (((1,), (1,)), ((), ())), preferred_element_type=F32)


def parts_of(a):
    high = a.astype(BF)
    return high, (a - high.astype(F32)).astype(BF)


def mul_fine(a, b):
    ah, al = parts_of(a)
    bh, bl = parts_of(b)
    return mul(jnp.concatenate([ah, al], 1), jnp.concatenate([bh, bh], 0)) + mul(ah, bl)


def grid_of(rows, cols, row0, col0):
    return (
        lax.broadcasted_iota(jnp.int32, (rows, cols), 0) + row0,
        lax.broadcasted_iota(jnp.int32, (rows, cols), 1) + col0,
    )


def first_of(place, starts_ref):
    begin = jnp.zeros_like(place)
    for n in range(starts_ref.shape[0]):
        begin = jnp.where(place >= starts_ref[n], starts_ref[n], begin)
    return begin


def directions(u, braw):
    scale = lax.rsqrt(jnp.sum(u * u, -1, keepdims=True) + EPS)
    wdir = u * scale
    beta = 2.0 * jax.nn.sigmoid(braw)
    return scale, wdir, beta


def unit_inverses(tiles):
    size = tiles[0].shape[0]
    row, col = grid_of(size, size, 0, 0)
    eye = jnp.where(row == col, 1.0, 0.0)
    near = (row // 8) == (col // 8)
    base = [jnp.where(near, n, 0.0) for n in tiles]
    two = [mul_fine(n, n) for n in base]
    three = [mul_fine(n, m) for n, m in zip(base, two)]
    four = [mul_fine(m, m) for m in two]
    low = [eye + a + b + c for a, b, c in zip(base, two, three)]
    done = [p + mul_fine(p, f) for p, f in zip(low, four)]
    span = 8
    while span < size:
        cross = ((row // (2 * span)) == (col // (2 * span))) & ((row // span) != (col // span))
        part = [mul_fine(jnp.where(cross, n, 0.0), d) for n, d in zip(tiles, done)]
        done = [d + mul_fine(d, p) for d, p in zip(done, part)]
        span *= 2
    return done


def solve_kernel(
    starts_ref,
    core_ref,
    nm_ref,
    np_ref,
    wu0_ref,
    wu1_ref,
    wk0_ref,
    wk1_ref,
    bias_ref,
    k_ref,
    u_ref,
    b_ref,
    c_ref,
    t_ref,
):
    length, cols = k_ref.shape
    heads = b_ref.shape[1]
    part = wu0_ref.shape[0]
    core = core_ref[0]
    block = nm_ref.shape[0] // 2
    for src, side in ((nm_ref, core), (np_ref, 1 - core)):
        a0, a1 = src[:, :part], src[:, part:]
        uk = mul(a0, wu0_ref[...]) + mul(a1, wu1_ref[...])
        keys = mul(a0, wk0_ref[...]) + mul(a1, wk1_ref[...])
        for n in range(2):
            there = pl.ds(pl.multiple_of((2 * n + side) * block, block), block)
            here = slice(n * block, (n + 1) * block)
            u_ref[there, :] = uk[here, :cols]
            b_ref[there, :] = uk[here, cols : cols + heads] + bias_ref[...]
            k_ref[there, :] = keys[here].astype(BF)
    dim = cols // heads
    half, tile = length // 2, length // 4
    row, col = grid_of(length, half, 0, 0)
    row1, col1 = grid_of(half, half, half, half)
    begin = first_of(lax.broadcasted_iota(jnp.int32, (length, 1), 0), starts_ref)
    strict_a = (col >= begin) & (col < row)
    strict_b = (col1 >= begin[half:]) & (col1 < row1)
    state = []
    tiles = []
    for h in range(heads):
        at = slice(h * dim, (h + 1) * dim)
        _, wdir, beta = directions(u_ref[:, at], b_ref[:, h : h + 1])
        wd, wb = wdir.astype(BF), (wdir * beta).astype(BF)
        la = jnp.where(strict_a, mul_t(wd, wb[:half]), 0.0)
        lb = jnp.where(strict_b, mul_t(wd[half:], wb[half:]), 0.0)
        state.append((wd, la, lb))
        tiles += [-la[:tile, :tile], -la[tile:half, tile:], -lb[:tile, :tile], -lb[tile:, tile:]]
    done = unit_inverses(tiles)
    for h in range(heads):
        at = slice(h * dim, (h + 1) * dim)
        wd, la, lb = state[h]
        whole = []
        for n, lower in enumerate((la[:half], lb)):
            d0, d1 = done[4 * h + 2 * n], done[4 * h + 2 * n + 1]
            d10 = -mul_fine(d1, mul_fine(lower[tile:, :tile], d0))
            t = jnp.concatenate(
                [jnp.concatenate([d0, jnp.zeros_like(d0)], 1), jnp.concatenate([d10, d1], 1)], 0
            )
            t_ref[h, n] = t.T.astype(BF)
            whole.append(t.astype(BF))
        k = k_ref[:, at]
        ra = jnp.where(strict_a, mul_t(wd, k[:half]), 0.0)
        rb = jnp.where(strict_b, mul_t(wd[half:], k[half:]), 0.0)
        c00 = mul(whole[0], ra[:half].astype(BF)).astype(BF)
        g10 = ra[half:] - mul(la[half:].astype(BF), c00)
        c1 = mul(whole[1], jnp.concatenate([g10, rb], 1).astype(BF)).astype(BF)
        c_ref[h, :half, :half] = c00
        c_ref[h, half:, :] = c1


def forward_kernel(
    starts_ref,
    core_ref,
    nm_ref,
    np_ref,
    qv0_ref,
    qv1_ref,
    wo0_ref,
    wo1_ref,
    k_ref,
    u_ref,
    b_ref,
    c_ref,
    q_ref,
    v_ref,
    o_ref,
    p_ref,
    keep_ref,
    send_ref,
):
    length, cols = q_ref.shape
    heads = b_ref.shape[1]
    part = qv0_ref.shape[0]
    core = core_ref[0]
    block = nm_ref.shape[0] // 2
    for src, side in ((nm_ref, core), (np_ref, 1 - core)):
        qv = mul(src[:, :part], qv0_ref[...]) + mul(src[:, part:], qv1_ref[...])
        for n in range(2):
            there = pl.ds(pl.multiple_of((2 * n + side) * block, block), block)
            here = slice(n * block, (n + 1) * block)
            q_ref[there, :] = qv[here, :cols].astype(BF)
            v_ref[there, :] = qv[here, cols:].astype(BF)
    dim = cols // heads
    half = length // 2
    soft = dim ** -0.5
    row, col = grid_of(length, half, 0, 0)
    row1, col1 = grid_of(half, half, half, half)
    begin = first_of(lax.broadcasted_iota(jnp.int32, (length, 1), 0), starts_ref)
    from_doc = col >= begin
    upto_a = from_doc & (col <= row)
    upto_b = (col1 >= begin[half:]) & (col1 <= row1)
    for h in range(heads):
        at = slice(h * dim, (h + 1) * dim)
        _, wdir, beta = directions(u_ref[:, at], b_ref[:, h : h + 1])
        wb = (wdir * beta).astype(BF)
        q, k, v = q_ref[:, at], k_ref[:, at], v_ref[:, at]
        c00, c1 = c_ref[h, :half, :half], c_ref[h, half:, :]
        xa = jnp.where(upto_a, mul_t(q, wb[:half]), 0.0).astype(BF)
        xb = jnp.where(upto_b, mul_t(q[half:], wb[half:]), 0.0).astype(BF)
        sa = mul_t(q, k[:half]) - mul(xa, c00)
        s0 = jnp.where(upto_a[:half], sa[:half], -1e30)
        low = mul(xb, c1)
        s10 = jnp.where(from_doc[half:], sa[half:] - low[:, :half], -1e30)
        s11 = jnp.where(upto_b, mul_t(q[half:], k[half:]) - low[:, half:], -1e30)
        top = jnp.max(s0, -1, keepdims=True)
        w = jnp.exp((s0 - top) * soft)
        w = (w * (1.0 / jnp.sum(w, -1, keepdims=True))).astype(BF)
        p_ref[h, :half, :half] = w
        o_ref[:half, at] = mul(w, v[:half]).astype(BF)
        s1 = jnp.concatenate([s10, s11], 1)
        top = jnp.max(s1, -1, keepdims=True)
        w = jnp.exp((s1 - top) * soft)
        w = (w * (1.0 / jnp.sum(w, -1, keepdims=True))).astype(BF)
        p_ref[h, half:, :] = w
        o_ref[half:, at] = mul(w, v).astype(BF)
    for n in range(2):
        here = slice(n * block, (n + 1) * block)
        for dst, side in ((send_ref, 1 - core), (keep_ref, core)):
            o = o_ref[pl.ds(pl.multiple_of((2 * n + side) * block, block), block), :]
            dst[here, :part] = mul(o, wo0_ref[...]).astype(dst.dtype)
            dst[here, part:] = mul(o, wo1_ref[...]).astype(dst.dtype)


def backward_kernel(
    starts_ref,
    core_ref,
    k_ref,
    u_ref,
    b_ref,
    c_ref,
    t_ref,
    q_ref,
    v_ref,
    p_ref,
    dm_ref,
    dp_ref,
    wo0_ref,
    wo1_ref,
    wu0_ref,
    wu1_ref,
    wk0_ref,
    wk1_ref,
    qv0_ref,
    qv1_ref,
    nm_ref,
    np_ref,
    duk_out,
    dqv_out,
    keep_ref,
    send_ref,
    gain_ref,
    do_ref,
    duk_ref,
    dqv_ref,
):
    part = wu0_ref.shape[0]
    wide = duk_ref.shape[1]
    near = wu0_ref.shape[1]
    core = core_ref[0]
    block = dm_ref.shape[0] // 2
    for src, side in ((dm_ref, core), (dp_ref, 1 - core)):
        d = mul_t(src[:, :part], wo0_ref[...]) + mul_t(src[:, part:], wo1_ref[...])
        for n in range(2):
            there = pl.ds(pl.multiple_of((2 * n + side) * block, block), block)
            do_ref[there, :] = d[n * block : (n + 1) * block].astype(BF)
    length = q_ref.shape[0]
    heads = b_ref.shape[1]
    dim = q_ref.shape[1] // heads
    half = length // 2
    soft = dim ** -0.5
    row, col = grid_of(length, half, 0, 0)
    row1, col1 = grid_of(half, half, half, half)
    begin = first_of(lax.broadcasted_iota(jnp.int32, (length, 1), 0), starts_ref)
    from_doc = col >= begin
    strict_a = from_doc & (col < row)
    upto_a = from_doc & (col <= row)
    strict_b = (col1 >= begin[half:]) & (col1 < row1)
    upto_b = (col1 >= begin[half:]) & (col1 <= row1)
    early, late = grid_of(half, length, 0, 0)
    begin_t = first_of(lax.broadcasted_iota(jnp.int32, (1, length), 1), starts_ref)
    from_doc_t = early >= begin_t
    upto_a_t = from_doc_t & (early <= late)
    early1, late1 = grid_of(half, half, half, half)
    upto_b_t = (early1 >= begin_t[:, half:]) & (early1 <= late1)
    dbraws = []
    for h in range(heads):
        at = slice(h * dim, (h + 1) * dim)
        scale, wdir, beta = directions(u_ref[:, at], b_ref[:, h : h + 1])
        wd, wb = wdir.astype(BF), (wdir * beta).astype(BF)
        q, k, v, do = q_ref[:, at], k_ref[:, at], v_ref[:, at], do_ref[:, at]
        qt, wdt, dot_ = q.T, wd.T, do.T
        p0, p1 = p_ref[h, :half, :half], p_ref[h, half:, :]
        c00, c1 = c_ref[h, :half, :half], c_ref[h, half:, :]
        t0, t1 = t_ref[h, 0], t_ref[h, 1]
        p0f, p1f = p0.astype(F32), p1.astype(F32)
        dp0 = mul_t(do[:half], v[:half])
        dp1 = mul_t(do[half:], v)
        ds0 = p0f * (dp0 - jnp.sum(p0f * dp0, -1, keepdims=True)) * soft
        ds1 = p1f * (dp1 - jnp.sum(p1f * dp1, -1, keepdims=True)) * soft
        ds0, ds1 = ds0.astype(BF), ds1.astype(BF)
        dsa = jnp.concatenate([ds0, ds1[:, :half]], 0)
        dxa = jnp.where(upto_a, mul_t(dsa, c00), 0.0).astype(BF)
        dxb = jnp.where(upto_b, mul_t(ds1, c1), 0.0).astype(BF)
        xta = jnp.where(upto_a_t, mul_t(wb[:half], q), 0.0).astype(BF)
        xtb = jnp.where(upto_b_t, mul_t(wb[half:], q[half:]), 0.0).astype(BF)
        lta = jnp.where(from_doc_t[:, half:], mul_t(wb[:half], wd[half:]), 0.0).astype(BF)
        dc00 = mul(xta, dsa)
        dc1 = mul(xtb, ds1).astype(BF)
        z1 = mul(t1, dc1)
        z10 = jnp.where(from_doc[half:], z1[:, :half], 0.0).astype(BF)
        z11 = jnp.where(strict_b, z1[:, half:], 0.0).astype(BF)
        z00 = mul(t0, (dc00 - mul(lta, z10)).astype(BF))
        z00 = jnp.where(strict_a[:half], z00, 0.0).astype(BF)
        za = jnp.concatenate([z00, z10], 0)
        z1 = jnp.concatenate([z10, z11], 1)
        dla = jnp.where(strict_a, mul_t(za, c00), 0.0).astype(BF)
        dlb = jnp.where(strict_b, mul_t(z1, c1), 0.0).astype(BF)
        dq0 = mul(ds0, k[:half]) - mul(dxa[:half], wb[:half])
        dq1 = mul(ds1, k) - mul(dxa[half:], wb[:half]) - mul(dxb, wb[half:])
        dk0 = mul(qt, dsa) - mul(wdt, za)
        dk1 = mul(qt[:, half:], ds1[:, half:]) - mul(wdt[:, half:], z11)
        y0 = mul(wdt, dla) - mul(qt, dxa)
        y1 = mul(wdt[:, half:], dlb) - mul(qt[:, half:], dxb)
        dv0 = mul(dot_[:, :half], p0) + mul(dot_[:, half:], p1[:, :half])
        dv1 = mul(dot_[:, half:], p1[:, half:])
        dw0 = mul(dla[:half], wb[:half]) - mul(z00, k[:half])
        dw1 = mul(dla[half:], wb[:half]) + mul(dlb, wb[half:]) - mul(z1, k)
        y = jnp.concatenate([y0, y1], 1).T
        dwd = beta * y + jnp.concatenate([dw0, dw1], 0)
        dbeta = jnp.sum(wdir * y, -1, keepdims=True)
        du = scale * (dwd - wdir * jnp.sum(wdir * dwd, -1, keepdims=True))
        dqv_ref[:half, at] = dq0.astype(BF)
        dqv_ref[half:, at] = dq1.astype(BF)
        dqv_ref[:, (heads + h) * dim : (heads + h + 1) * dim] = (
            jnp.concatenate([dv0, dv1], 1).T.astype(BF)
        )
        duk_ref[:, at] = du.astype(BF)
        behind = wide - heads * dim
        duk_ref[:, behind + h * dim : behind + (h + 1) * dim] = (
            jnp.concatenate([dk0, dk1], 1).T.astype(BF)
        )
        dbraws.append(dbeta * beta * (1.0 - 0.5 * beta))
    lane = lax.broadcasted_iota(jnp.int32, (length, wide - 2 * heads * dim), 1)
    last = jnp.zeros(lane.shape, F32)
    for h in range(heads):
        last = jnp.where(lane == h, dbraws[h], last)
    duk_ref[:, heads * dim : wide - heads * dim] = last.astype(BF)
    gain = [0.0, 0.0]
    for dst, norm, side, base in (
        (send_ref, np_ref, 1 - core, 2 * block),
        (keep_ref, nm_ref, core, 0),
    ):
        for n in range(2):
            there = pl.ds(pl.multiple_of((2 * n + side) * block, block), block)
            here = slice(base + n * block, base + (n + 1) * block)
            duk, dqv = duk_ref[there, :], dqv_ref[there, :]
            duk_out[here, :] = duk
            dqv_out[here, :] = dqv
            rows = slice(n * block, (n + 1) * block)
            du, dk = duk[:, :near], duk[:, near:]
            for i, (cut, wu, wk, qv) in enumerate(
                (
                    (slice(0, part), wu0_ref, wk0_ref, qv0_ref),
                    (slice(part, 2 * part), wu1_ref, wk1_ref, qv1_ref),
                )
            ):
                dn = mul_t(du, wu[...]) + mul_t(dk, wk[...]) + mul_t(dqv, qv[...])
                dst[rows, cut] = dn.astype(dst.dtype)
                gain[i] += jnp.sum(dn * norm[rows, cut].astype(F32), 0, keepdims=True)
    gain_ref[:, :part] = gain[0]
    gain_ref[:, part:] = gain[1]


def vmem(n):
    return [pl.BlockSpec(memory_space=pltpu.VMEM)] * n


def smem(n):
    return [pl.BlockSpec(memory_space=pltpu.SMEM)] * n


def shape_of(*dims, kind=BF):
    return jax.ShapeDtypeStruct(dims, kind)


def params(mib=48):
    return pltpu.CompilerParams(vmem_limit_bytes=mib * 2**20)


def cost(us):
    return pl.CostEstimate(flops=int(us * 3e8), bytes_accessed=1000, transcendentals=0)


def attn_solve(starts, core, nm, np_, wu0, wu1, wk0, wk1, bias):
    length, heads = 2 * nm.shape[0], bias.shape[1]
    cols = wk0.shape[1]
    half = length // 2
    return pl.pallas_call(
        solve_kernel,
        in_specs=smem(2) + vmem(7),
        out_specs=vmem(5),
        out_shape=[
            shape_of(length, cols),
            shape_of(length, cols, kind=F32),
            shape_of(length, heads, kind=F32),
            shape_of(heads, length, length),
            shape_of(heads, 2, half, half),
        ],
        compiler_params=params(),
        cost_estimate=cost(12),
        name="attn_solve",
    )(starts, core, nm, np_, wu0, wu1, wk0, wk1, bias)


def attn_forward(starts, core, nm, np_, qv0, qv1, wo0, wo1, k, u, braw, c):
    length, cols = k.shape
    half, width, heads = length // 2, nm.shape[1], braw.shape[1]
    return pl.pallas_call(
        forward_kernel,
        in_specs=smem(2) + vmem(10),
        out_specs=vmem(6),
        out_shape=[
            shape_of(length, cols),
            shape_of(length, cols),
            shape_of(length, cols),
            shape_of(heads, length, length),
            shape_of(half, width, kind=F32),
            shape_of(half, width),
        ],
        compiler_params=params(),
        cost_estimate=cost(9),
        name="attn_forward",
    )(starts, core, nm, np_, qv0, qv1, wo0, wo1, k, u, braw, c)


def attn_backward(starts, core, saved, dm, dp, *weights_and_norms):
    length, cols = saved[0].shape
    half, width = length // 2, dm.shape[1]
    near, far = weights_and_norms[2].shape[1], weights_and_norms[4].shape[1]
    return pl.pallas_call(
        backward_kernel,
        in_specs=smem(2) + vmem(20),
        out_specs=vmem(5),
        out_shape=[
            shape_of(length, near + far),
            shape_of(length, 2 * cols),
            shape_of(half, width, kind=F32),
            shape_of(half, width),
            shape_of(1, width, kind=F32),
        ],
        scratch_shapes=[
            pltpu.VMEM((length, cols), BF),
            pltpu.VMEM((length, near + far), BF),
            pltpu.VMEM((length, 2 * cols), BF),
        ],
        compiler_params=params(),
        cost_estimate=cost(21),
        name="attn_backward",
    )(starts, core, *saved, dm, dp, *weights_and_norms)


def feed_kernel(a_ref, w0_ref, w1_ref, keep_ref, send_ref):
    rows = a_ref.shape[0] // 2
    part = w0_ref.shape[1]
    for dst, at in ((send_ref, slice(rows, None)), (keep_ref, slice(0, rows))):
        dst[0, :, :part] = mul(a_ref[at, :], w0_ref[...]).astype(dst.dtype)
        dst[0, :, part:] = mul(a_ref[at, :], w1_ref[...]).astype(dst.dtype)


def ffn_feed(act, wd0, wd1):
    hidden, part = wd0.shape
    micros, rows = 2, act.shape[0] // 4
    weight = pl.BlockSpec((hidden, part), lambda m: (0, 0))
    out = pl.BlockSpec((1, rows, 2 * part), lambda m: (m, 0, 0))
    return pl.pallas_call(
        feed_kernel,
        grid=(micros,),
        in_specs=[pl.BlockSpec((2 * rows, hidden), lambda m: (m, 0)), weight, weight],
        out_specs=[out, out],
        out_shape=[
            shape_of(micros, rows, 2 * part, kind=F32),
            shape_of(micros, rows, 2 * part),
        ],
        compiler_params=params(),
        cost_estimate=cost(6),
        name="ffn_feed",
    )(act, wd0, wd1)


def ffn_grad_kernel(*refs):
    a, b = refs[:4], refs[4:6]
    own_ref, far_ref, turned = refs[6:]
    rows = a[0].shape[0]
    part = own_ref.shape[0]

    @pl.when(pl.program_id(0) == 0)
    def _():
        for p in range(4):
            turned[:, p * rows : (p + 1) * rows] = a[p][...].T

    out = mul(turned[:, : 2 * rows], b[0][...]) + mul(turned[:, 2 * rows :], b[1][...])
    own_ref[...] = out[:part]
    far_ref[...] = out[part:].astype(BF)


def ffn_grad(a, b, tile=256):
    rows, width = a[0].shape
    hidden = b[0].shape[1]
    whole = pl.BlockSpec((rows, width), lambda i: (0, 0))
    cols = pl.BlockSpec((2 * rows, tile), lambda i: (0, i))
    out = pl.BlockSpec((width // 2, tile), lambda i: (0, i))
    return pl.pallas_call(
        ffn_grad_kernel,
        grid=(hidden // tile,),
        in_specs=[whole] * 4 + [cols] * 2,
        out_specs=[out, out],
        out_shape=[shape_of(width // 2, hidden, kind=F32), shape_of(width // 2, hidden)],
        scratch_shapes=[pltpu.VMEM((width, 4 * rows), BF)],
        compiler_params=params(),
        cost_estimate=cost(6),
        name="ffn_grad",
    )(*a, *b)


def attn_grad_kernel(core_ref, *refs):
    a, d, dqv, duk, attn = refs[:4], refs[4:8], refs[8:10], refs[10:12], refs[12:14]
    extra, own, far = refs[14:16], refs[16:18], refs[18:20]
    turned, turned_d, placed = refs[20:]
    rows = a[0].shape[0]
    block = rows // 2
    part = own[0].shape[0]
    cols = attn[0].shape[1]
    for p in range(4):
        here = slice(p * rows, (p + 1) * rows)
        turned[:, here] = a[p][...].T
        turned_d[:, here] = d[p][...].T
        side = core_ref[0] if p % 2 == 0 else 1 - core_ref[0]
        for n in range(2):
            there = pl.ds(pl.multiple_of((2 * n + side) * block, block), block)
            placed[p * rows + n * block : p * rows + (n + 1) * block, :] = attn[p // 2][there, :]
    ends = [0]
    for o in own:
        ends.append(ends[-1] + o.shape[1])
    pieces = [(cols, cols, 128, duk, 0)]
    at = cols + 128
    for src, begin, size in ((dqv, 0, 2 * cols), (duk, cols + 128, cols), (duk, 0, cols)):
        while size:
            i = max(n for n in range(len(own)) if ends[n] <= at)
            n = min(size, ends[i + 1] - at)
            pieces.append((at - ends[i], begin, n, src, i))
            at, begin, size = at + n, begin + n, size - n
    for side, dsts in ((1, far), (0, own)):
        half = slice(side * part, (side + 1) * part)
        dsts[0][:, :cols] = mul(turned_d[half, :], placed[...]).astype(dsts[0].dtype)
        for to, begin, n, src, i in pieces:
            out = mul(turned[half, : 2 * rows], src[0][:, begin : begin + n])
            out = out + mul(turned[half, 2 * rows :], src[1][:, begin : begin + n])
            if i == 0 and to == cols:
                out = out + extra[side][...]
            dsts[i][:, to : to + n] = out.astype(dsts[i].dtype)


def attn_grad(core, a, d, dqv, duk, attn, extra):
    rows, width = a[0].shape
    part, cols = width // 2, attn[0].shape[1]
    wide = cols + 128
    sizes = (2 * wide,) * 2
    out = pl.pallas_call(
        attn_grad_kernel,
        in_specs=smem(1) + vmem(16),
        out_specs=vmem(4),
        out_shape=[shape_of(part, n, kind=F32) for n in sizes] + [shape_of(part, n) for n in sizes],
        scratch_shapes=[
            pltpu.VMEM((width, 4 * rows), BF),
            pltpu.VMEM((width, 4 * rows), BF),
            pltpu.VMEM((4 * rows, cols), BF),
        ],
        compiler_params=params(),
        cost_estimate=cost(14),
        name="attn_grad",
    )(core, *a, *d, *dqv, *duk, *attn, *extra)
    return list(zip(out[:2], out[2:]))


def up_kernel(*refs):
    n2, g = refs[:4], refs[4:8]
    wg0, wg1, wu0, wu1, one_ref, two_ref, act_ref, own_ref, far_ref = refs[8:]
    part = wg0.shape[0]
    rows = n2[0].shape[0]
    total = 0.0
    for p in range(4):
        a0, a1 = n2[p][:, :part], n2[p][:, part:]
        gate = mul(a0, wg0[...]) + mul(a1, wg1[...])
        upper = mul(a0, wu0[...]) + mul(a1, wu1[...])
        sigma = jax.nn.sigmoid(gate)
        swish = gate * sigma
        act = (swish * upper).astype(BF)
        at = slice(p * rows, (p + 1) * rows)
        one_ref[at, :] = (upper * sigma * (1.0 + gate * (1.0 - sigma))).astype(BF)
        two_ref[at, :] = swish.astype(BF)
        act_ref[at, :] = act
        total = total + mul(act.T, g[p][...])
    own_ref[...] = total[:, :part]
    far_ref[...] = total[:, part:].astype(BF)


def ffn_up(n2, g, wg0, wg1, wu0, wu1, tile=256):
    rows, width = n2[0].shape
    part, hidden = wg0.shape
    whole = pl.BlockSpec((rows, width), lambda i: (0, 0))
    cols = pl.BlockSpec((part, tile), lambda i: (0, i))
    tall = pl.BlockSpec((4 * rows, tile), lambda i: (0, i))
    flat = pl.BlockSpec((tile, part), lambda i: (i, 0))
    return pl.pallas_call(
        up_kernel,
        grid=(hidden // tile,),
        in_specs=[whole] * 8 + [cols] * 4,
        out_specs=[tall] * 3 + [flat] * 2,
        out_shape=[shape_of(4 * rows, hidden)] * 3
        + [shape_of(hidden, part, kind=F32), shape_of(hidden, part)],
        compiler_params=params(),
        cost_estimate=cost(16),
        name="ffn_up",
    )(*n2, *g, wg0, wg1, wu0, wu1)


def down_kernel(*refs):
    g, one_ref, two_ref = refs[:2], refs[2], refs[3]
    wd0, wd1, wg0, wg1, wu0, wu1, dg_ref, du_ref, keep_ref, send_ref, acc = refs[4:]
    part = wg0.shape[0]
    rows = g[0].shape[0]
    step = pl.program_id(0)

    for p in range(2):
        d = mul_t(g[p][:, :part], wd0[...]) + mul_t(g[p][:, part:], wd1[...])
        at = slice(p * rows, (p + 1) * rows)
        dg = (d * one_ref[at, :].astype(F32)).astype(BF)
        du = (d * two_ref[at, :].astype(F32)).astype(BF)
        dg_ref[at, :] = dg
        du_ref[at, :] = du
        new0 = mul_t(dg, wg0[...]) + mul_t(du, wu0[...])
        new1 = mul_t(dg, wg1[...]) + mul_t(du, wu1[...])

        @pl.when(step == 0)
        def _():
            acc[at, :part] = new0
            acc[at, part:] = new1

        @pl.when(step > 0)
        def _():
            acc[at, :part] += new0
            acc[at, part:] += new1

    @pl.when(step == pl.num_programs(0) - 1)
    def _():
        keep_ref[...] = acc[:rows, :]
        send_ref[...] = acc[rows:, :].astype(BF)


def ffn_down(m, g, one, two, wd0, wd1, wg0, wg1, wu0, wu1, tile=256):
    rows, width = g[0].shape
    part, hidden = wg0.shape
    whole = pl.BlockSpec((rows, width), lambda i: (0, 0))
    cols = pl.BlockSpec((part, tile), lambda i: (0, i))
    flat = pl.BlockSpec((tile, part), lambda i: (i, 0))
    pick_m = pl.BlockSpec((2 * rows, tile), lambda i: (m, i))
    tall = pl.BlockSpec((2 * rows, tile), lambda i: (0, i))
    return pl.pallas_call(
        down_kernel,
        grid=(hidden // tile,),
        in_specs=[whole] * 2 + [pick_m] * 2 + [flat] * 2 + [cols] * 4,
        out_specs=[tall] * 2 + [whole] * 2,
        out_shape=[shape_of(2 * rows, hidden)] * 2
        + [shape_of(rows, width, kind=F32), shape_of(rows, width)],
        scratch_shapes=[pltpu.VMEM((2 * rows, width), F32)],
        compiler_params=params(),
        cost_estimate=cost(13),
        name="ffn_down",
    )(*g, one, two, wd0, wd1, wg0, wg1, wu0, wu1)


def swap_wid(a):
    return lax.ppermute(a, "wid", [(0, 1), (1, 0)])


def swap_core(a):
    return lax.ppermute(a, "hid", [(0, 1), (1, 0), (2, 3), (3, 2)])


def swap_chip(a):
    return lax.ppermute(a, "hid", [(0, 2), (2, 0), (1, 3), (3, 1)])


def tie(a, *others):
    return lax.optimization_barrier((a, *others))[0]


class RowSum:
    def __init__(self, a):
        self.value = a
        self.line = lax.axis_size("rows") == 4
        self.stage = 0

    def send(self):
        self.stage += 1
        if self.line and self.stage <= 3:
            moves = {1: [(0, 1), (3, 2)], 2: [(1, 2), (2, 1)], 3: [(1, 0), (2, 3)]}
            self.got = lax.ppermute(self.value, "rows", moves[self.stage])

    def take(self, then):
        if not self.line:
            if self.stage == 3:
                self.value = lax.psum(then(self.value), "rows").astype(F32)
        elif self.stage < 3:
            self.value = (self.value.astype(F32) + then(self.got).astype(F32)).astype(BF)
        else:
            place = lax.axis_index("rows")
            inner = (place == 1) | (place == 2)
            self.value = jnp.where(inner, self.value, then(self.got)).astype(F32)


def pick(pair, first):
    a, b = pair
    return jnp.where(first, a, b), jnp.where(first, b, a)

ORDER = (
    "fd0", "low0", "fd1", "low1", "gF", "dL", "dmid0", "ab0", "gL", "dM",
    "dmid1", "uF", "ab1", "dW", "gM", "aF", "uL", "vL", "aL", "bL",
    "uM", "gW", "dE", "vM", "feed", "cL", "eL", "aM", "uW", "gE",
    "bM", "vW", "uE", "flow", "cM", "vE", "aW", "eM", "dlow", "bW",
    "aE", "outs", "cW", "bE", "dxs", "eW", "s1", "cE", "s2", "outsf",
    "s3", "dxsf", "eE",
)


def on_device(
    inputs,
    starts,
    norm_one,
    w_query,
    w_key,
    w_value,
    w_house,
    strength_weight,
    b_beta,
    w_out,
    norm_two,
    gate_weight,
    up_weight,
    w_down,
    cotangent,
):
    micros, _, block, part = inputs.shape
    width = 2 * part
    half = 2 * block
    cols = w_query.shape[1]
    heads = strength_weight.shape[1]
    wid = lax.axis_index("wid")
    hid = lax.axis_index("hid")
    core, chip = hid % 2, hid // 2
    chip0, wid0 = chip == 0, wid == 0
    core_arg = core.astype(jnp.int32).reshape(1)

    def take(a, axis, index):
        return lax.dynamic_index_in_dim(a, index, axis, keepdims=False)

    def assisted(w, *before):
        size = w.shape[0] // lax.axis_size("rows")
        share = lax.dynamic_slice_in_dim(w, lax.axis_index("rows") * size, size)
        got = swap_wid(tie(share, *before))
        return lax.all_gather(got, "rows", axis=0, tiled=True), got

    x_far = swap_wid(take(inputs, 1, 1 - wid))
    gains = jnp.stack([norm_one, norm_two])
    gains_far = swap_wid(gains)
    gains = jnp.concatenate([gains, gains_far], 1)
    w_u = jnp.concatenate([w_house, strength_weight, jnp.zeros((part, 128 - heads), BF)], 1)
    w_qv = jnp.concatenate([w_query, w_value], 1)
    u_far = swap_wid(tie(w_u, x_far))
    k_far = swap_wid(tie(w_key, x_far))
    up_far, up_share = assisted(up_weight, u_far)
    down_far, down_share = assisted(w_down, k_far)
    qv_far = swap_wid(tie(w_qv, u_far))
    g_far = swap_wid(tie(take(cotangent, 1, 1 - wid), k_far))
    out_far = swap_wid(tie(w_out, k_far))
    row_starts = take(starts, 1, wid)

    def gather_chip(mine, far):
        mine = jnp.concatenate([mine, far], -1)
        a, b = pick((mine, swap_chip(mine)), chip0)
        return jnp.stack([a, b], 1).reshape(micros, half, width)

    def chip_sum(keep, send):
        return keep + swap_core(send).astype(F32)

    def my_block(a):
        return take(a.reshape(2, block, a.shape[-1]), 0, chip)

    x_half = tie(gather_chip(take(inputs, 1, wid), x_far), u_far).astype(F32)
    scale_one = lax.rsqrt(jnp.mean(x_half * x_half, -1, keepdims=True) + EPS)
    nm_half = (x_half * scale_one * gains[0]).astype(BF)
    nm_half = tie(nm_half, k_far)
    nm_peer = swap_core(nm_half)
    saved, attns, mids, scales, n2_parts = [], [], [], [], []
    uk_w = (w_u, u_far, w_key, k_far)
    for m in range(micros):
        nm = nm_half[m] if m == 0 else tie(nm_half[m], saved[0][0])
        saved.append(attn_solve(row_starts[m], core_arg, nm, nm_peer[m], *uk_w, b_beta[None]))
    g_half = gather_chip(tie(take(cotangent, 1, wid), saved[-1][0]), g_far)
    def finish_mid(m, low, got):
        mid = x_half[m] + low.astype(F32) + got.astype(F32)
        scale_two = lax.rsqrt(jnp.mean(mid * mid, -1, keepdims=True) + EPS)
        n2 = (mid * scale_two * gains[1]).astype(BF)
        n2_parts.extend([n2, swap_core(n2)])
        mids.append(mid)
        scales.append(scale_two)

    low = saved[1][0]
    for m in range(micros):
        k, u, braw, c, t = saved[m]
        nm = tie(nm_half[m], low)
        q, v, attn, p, keep, send = attn_forward(
            row_starts[m], core_arg, nm, nm_peer[m], w_qv, qv_far, w_out, out_far, k, u, braw, c
        )
        saved[m] = (*saved[m], q, v, p)
        attns.append(attn)
        got = swap_core(send)
        if m == 1:
            finish_mid(0, low, tie(chip_got, keep))
            got = tie(got, n2_parts[0])
        low = (keep + got.astype(F32)).astype(BF)
        chip_got = swap_chip(low)
    finish_mid(1, low, chip_got)
    g_peer = swap_core(tie(g_half, low))
    g_parts = [a for m in range(micros) for a in (g_half[m], g_peer[m])]
    gate_far = swap_wid(tie(gate_weight, saved[1][0]))
    ffn_w = (gate_weight, gate_far, up_weight, up_far)
    one, two, act, down_own, down_far_part = ffn_up(n2_parts, g_parts, *ffn_w)
    ready = {"d": (down_own, swap_wid(down_far_part), slice(None))}

    last = [act]

    def then(a):
        return tie(a, last[0])

    def mark(a):
        last[0] = a
        return a

    s = {}
    steps = {}

    def stack_m(name):
        return jnp.concatenate([s[name + "0"], s[name + "1"]], 0)

    def row_steps(m, tag):
        def ffn_back():
            gm = (then(g_parts[2 * m]), g_parts[2 * m + 1])
            dg, du, keep, send = ffn_down(m, gm, one, two, w_down, down_far, *ffn_w)
            s["dg" + tag], s["du" + tag], s["nk" + tag] = mark(dg), du, keep
            s["ng" + tag] = swap_core(send)

        def low():
            s["nl" + tag] = mark((s["nk" + tag] + then(s["ng" + tag]).astype(F32)).astype(BF))
            s["nx" + tag] = swap_chip(s["nl" + tag])

        def d_mid():
            mid, scale = mids[m], scales[m]
            dn = s["nl" + tag].astype(F32) + then(s["nx" + tag]).astype(F32)
            inner = jnp.mean(mid * gains[1] * dn, -1, keepdims=True)
            d = g_half[m].astype(F32) + scale * gains[1] * dn
            d = d - mid * scale * scale * scale * inner
            s["d" + tag] = d
            s["g2" + tag] = 0.5 * jnp.sum(dn * mid * scale, 0)
            s["dl" + tag] = mark(d.astype(BF))
            s["dp" + tag] = swap_core(s["dl" + tag])

        def attn_back():
            duk, dqv, keep, send, s["g1" + tag] = attn_backward(
                row_starts[m],
                core_arg,
                saved[m],
                then(s["dl" + tag]),
                s["dp" + tag],
                w_out,
                out_far,
                *uk_w,
                w_qv,
                qv_far,
                nm_half[m],
                nm_peer[m],
            )
            s["duk" + tag], s["dqv" + tag], s["ak" + tag] = mark(duk), dqv, keep
            s["ag" + tag] = swap_core(send)

        steps["fd" + tag] = ffn_back
        steps["low" + tag] = low
        steps["dmid" + tag] = d_mid
        steps["ab" + tag] = attn_back

    for m in range(micros):
        row_steps(m, str(m))

    def grad_steps(name):
        state = {}

        def low():
            own, near, part_of = ready[name]
            near = then(near)[:, part_of].astype(F32)
            state["sum"] = RowSum(mark((own[:, part_of] + near).astype(BF)))
            state["sum"].send()

        def more():
            state["sum"].take(then)
            mark(state["sum"].value)
            state["sum"].send()

        def end():
            more()
            s[name] = state["sum"].value

        steps[name + "L"] = low
        steps[name + "M"] = more
        steps[name + "W"] = more
        steps[name + "E"] = end

    for name in "dguvabce":
        grad_steps(name)

    def put_ready(names, own, near):
        size = own.shape[1] // len(names)
        for n, name in enumerate(names):
            ready[name] = (own, near, slice(n * size, (n + 1) * size))

    def ffn_grad_step(name, of):
        def step():
            norms = (then(n2_parts[0]), *n2_parts[1:])
            b = (s[of + "0"], s[of + "1"])
            own, far = ffn_grad(norms, b)
            put_ready(name, own, swap_wid(mark(far)))

        return step

    steps["gF"] = ffn_grad_step("g", "dg")
    steps["uF"] = ffn_grad_step("uv", "du")

    def feed_step():
        keep, send = ffn_feed(then(act), w_down, down_far)
        mark(keep)
        for m in range(micros):
            s[f"fk{m}"], s[f"fg{m}"] = keep[m], swap_core(send[m])

    steps["feed"] = feed_step

    def attn_grad_step():
        duk = [s["duk0"], s["duk1"]]
        bias = sum(jnp.sum(a[:, cols : cols + heads].astype(F32), 0) for a in duk)
        scales = jnp.stack([(s["g10"] + s["g11"])[0] / gains[0], s["g20"] + s["g21"]], 1)
        column = lax.broadcasted_iota(jnp.int32, (width, 128), 1)
        row = lax.broadcasted_iota(jnp.int32, (width, 128), 0) % part
        extra = jnp.where(column == 2 * heads, scales[:, :1], 0.0)
        extra = extra + jnp.where(column == 2 * heads + 1, scales[:, 1:], 0.0)
        bias = jnp.pad(bias[None], ((0, 0), (heads, 128 - 2 * heads)))
        extra = extra + jnp.where(row == 0, bias, 0.0)
        norms = [a for m in range(micros) for a in (nm_half[m], nm_peer[m])]
        norms[0] = then(norms[0])
        dqv = [s["dqv0"], s["dqv1"]]
        db = [s["dl0"], s["dp0"], s["dl1"], s["dp1"]]
        pairs = attn_grad(core_arg, norms, db, dqv, duk, attns, (extra[:part], extra[part:]))
        mark(pairs[0][1])
        for names, (own, far) in zip(("ab", "ce"), pairs):
            put_ready(names, own, swap_wid(far))

    steps["aF"] = attn_grad_step

    def own_blocks(a):
        return jnp.stack([my_block(m) for m in a])

    def block_low(keep, got, name):
        def step():
            low = [s[keep + t] + then(s[got + t]).astype(F32) for t in ("0", "1")]
            low = jnp.stack(low).reshape(micros, 2, block, width)
            s[name + "l"] = take(low, 1, chip)
            s[name + "x"] = swap_chip(mark(take(low, 1, 1 - chip).astype(BF)))

        return step

    def rows_back(values, kind, name):
        own = values[..., :part].astype(kind)
        far = swap_wid(mark(values[..., part:].astype(BF)))

        def finish():
            a, b = pick((own, then(far).astype(kind)), wid0)
            s[name] = mark(jnp.stack([a, b], 1))

        steps[name + "f"] = finish

    def out_step():
        rows_back(own_blocks(mids) + s["fl"] + then(s["fx"]).astype(F32), BF, "outs")

    def dx_step():
        dn = s["al"] + then(s["ax"]).astype(F32)
        x, scale = own_blocks(x_half), own_blocks(scale_one)
        inner = jnp.mean(x * gains[0] * dn, -1, keepdims=True)
        dx = own_blocks([s["d0"], s["d1"]]) + scale * gains[0] * dn
        rows_back(dx - x * scale * scale * scale * inner, F32, "dxs")

    def small_core():
        s["few"] = then(s["a"])[:, cols + 2 * heads : cols + 2 * heads + 2]
        s["few_got"] = swap_core(s["few"])

    def small_chip():
        s["few"] = mark(s["few"] + then(s["few_got"]))
        s["few_got"] = swap_chip(s["few"])

    def small_end():
        s["small"] = mark(s["few"] + then(s["few_got"]))

    steps["s1"], steps["s2"], steps["s3"] = small_core, small_chip, small_end
    steps["flow"] = block_low("fk", "fg", "f")
    steps["dlow"] = block_low("ak", "ag", "a")
    steps["outs"] = out_step
    steps["dxs"] = dx_step
    for name in ORDER:
        steps[name]()
    outs, dxs = s["outs"], s["dxs"]
    g_down, g_gate, g_up = s["d"], s["g"], jnp.concatenate([s["u"], s["v"]], 1)
    g_out = s["a"][:, :cols].T
    strengths = s["a"][:, cols:]
    chunks = (s["b"], s["c"], s["e"])
    wide = cols + 128

    def columns(begin):
        out = []
        done = 0
        while done < cols:
            at = begin + done
            n = min(cols - done, wide - at % wide)
            out.append(chunks[at // wide][:, at % wide : at % wide + n])
            done += n
        return jnp.concatenate(out, 1)

    g_q, g_v, g_k, g_u = [columns(n * cols) for n in range(4)]
    return (
        outs,
        dxs,
        s["small"][:, 0],
        g_q,
        g_k,
        g_v,
        g_u,
        strengths[:, :heads],
        strengths[0, heads : 2 * heads],
        g_out,
        s["small"][:, 1],
        g_gate,
        g_up,
        g_down,
    )


def solution(mesh):
    tokens = P(None, "rows", "hid", "wid")
    tall, flat = P("wid", "hid"), P("hid", "wid")
    specs = (P("wid"), tall, tall, tall, tall, tall, P("hid"), flat, P("wid"), tall, tall, flat)
    return jax.shard_map(
        on_device,
        mesh=mesh,
        in_specs=(tokens, P(None, "rows", None), *specs, tokens),
        out_specs=(tokens, tokens, *specs),
        check_vma=False,
    )
```

```python
import jax
import jax.numpy as jnp
from jax import lax
from jax.experimental import pallas as pl
from jax.experimental.pallas import tpu as pltpu
from jax.sharding import PartitionSpec as P

EPS = 1e-06
F32 = jnp.float32
BF = jnp.bfloat16


def mul(a, b):
    return lax.dot_general(a, b, (((1,), (0,)), ((), ())), preferred_element_type=F32)


def mul_t(a, b):
    return lax.dot_general(a, b, (((1,), (1,)), ((), ())), preferred_element_type=F32)


def parts_of(a):
    high = a.astype(BF)
    return high, (a - high.astype(F32)).astype(BF)


def mul_fine(a, b):
    ah, al = parts_of(a)
    bh, bl = parts_of(b)
    return mul(jnp.concatenate([ah, al], 1), jnp.concatenate([bh, bh], 0)) + mul(ah, bl)


def grid_of(rows, cols, row0, col0):
    return (
        lax.broadcasted_iota(jnp.int32, (rows, cols), 0) + row0,
        lax.broadcasted_iota(jnp.int32, (rows, cols), 1) + col0,
    )


def first_of(place, starts_ref):
    begin = jnp.zeros_like(place)
    for n in range(starts_ref.shape[0]):
        begin = jnp.where(place >= starts_ref[n], starts_ref[n], begin)
    return begin


def directions(u, braw):
    scale = lax.rsqrt(jnp.sum(u * u, -1, keepdims=True) + EPS)
    wdir = u * scale
    beta = 2.0 * jax.nn.sigmoid(braw)
    return scale, wdir, beta


def unit_inverses(tiles):
    size = tiles[0].shape[0]
    row, col = grid_of(size, size, 0, 0)
    eye = jnp.where(row == col, 1.0, 0.0)
    near = (row // 8) == (col // 8)
    base = [jnp.where(near, n, 0.0) for n in tiles]
    two = [mul_fine(n, n) for n in base]
    three = [mul_fine(n, m) for n, m in zip(base, two)]
    four = [mul_fine(m, m) for m in two]
    low = [eye + a + b + c for a, b, c in zip(base, two, three)]
    done = [p + mul_fine(p, f) for p, f in zip(low, four)]
    span = 8
    while span < size:
        cross = ((row // (2 * span)) == (col // (2 * span))) & ((row // span) != (col // span))
        part = [mul_fine(jnp.where(cross, n, 0.0), d) for n, d in zip(tiles, done)]
        done = [d + mul_fine(d, p) for d, p in zip(done, part)]
        span *= 2
    return done


def solve_kernel(
    starts_ref,
    core_ref,
    nm_ref,
    np_ref,
    wu0_ref,
    wu1_ref,
    wk0_ref,
    wk1_ref,
    bias_ref,
    k_ref,
    u_ref,
    b_ref,
    c_ref,
    t_ref,
):
    length, cols = k_ref.shape
    heads = b_ref.shape[1]
    part = wu0_ref.shape[0]
    core = core_ref[0]
    block = nm_ref.shape[0] // 2
    for src, side in ((nm_ref, core), (np_ref, 1 - core)):
        a0, a1 = src[:, :part], src[:, part:]
        uk = mul(a0, wu0_ref[...]) + mul(a1, wu1_ref[...])
        keys = mul(a0, wk0_ref[...]) + mul(a1, wk1_ref[...])
        for n in range(2):
            there = pl.ds(pl.multiple_of((2 * n + side) * block, block), block)
            here = slice(n * block, (n + 1) * block)
            u_ref[there, :] = uk[here, :cols]
            b_ref[there, :] = uk[here, cols : cols + heads] + bias_ref[...]
            k_ref[there, :] = keys[here].astype(BF)
    dim = cols // heads
    half, tile = length // 2, length // 4
    row, col = grid_of(length, half, 0, 0)
    row1, col1 = grid_of(half, half, half, half)
    begin = first_of(lax.broadcasted_iota(jnp.int32, (length, 1), 0), starts_ref)
    strict_a = (col >= begin) & (col < row)
    strict_b = (col1 >= begin[half:]) & (col1 < row1)
    state = []
    tiles = []
    for h in range(heads):
        at = slice(h * dim, (h + 1) * dim)
        _, wdir, beta = directions(u_ref[:, at], b_ref[:, h : h + 1])
        wd, wb = wdir.astype(BF), (wdir * beta).astype(BF)
        la = jnp.where(strict_a, mul_t(wd, wb[:half]), 0.0)
        lb = jnp.where(strict_b, mul_t(wd[half:], wb[half:]), 0.0)
        state.append((wd, la, lb))
        tiles += [-la[:tile, :tile], -la[tile:half, tile:], -lb[:tile, :tile], -lb[tile:, tile:]]
    done = unit_inverses(tiles)
    for h in range(heads):
        at = slice(h * dim, (h + 1) * dim)
        wd, la, lb = state[h]
        whole = []
        for n, lower in enumerate((la[:half], lb)):
            d0, d1 = done[4 * h + 2 * n], done[4 * h + 2 * n + 1]
            d10 = -mul_fine(d1, mul_fine(lower[tile:, :tile], d0))
            t = jnp.concatenate(
                [jnp.concatenate([d0, jnp.zeros_like(d0)], 1), jnp.concatenate([d10, d1], 1)], 0
            )
            t_ref[h, n] = t.T.astype(BF)
            whole.append(t.astype(BF))
        k = k_ref[:, at]
        ra = jnp.where(strict_a, mul_t(wd, k[:half]), 0.0)
        rb = jnp.where(strict_b, mul_t(wd[half:], k[half:]), 0.0)
        c00 = mul(whole[0], ra[:half].astype(BF)).astype(BF)
        g10 = ra[half:] - mul(la[half:].astype(BF), c00)
        c1 = mul(whole[1], jnp.concatenate([g10, rb], 1).astype(BF)).astype(BF)
        c_ref[h, :half, :half] = c00
        c_ref[h, half:, :] = c1


def forward_kernel(
    starts_ref,
    core_ref,
    nm_ref,
    np_ref,
    qv0_ref,
    qv1_ref,
    wo0_ref,
    wo1_ref,
    k_ref,
    u_ref,
    b_ref,
    c_ref,
    q_ref,
    v_ref,
    o_ref,
    p_ref,
    keep_ref,
    send_ref,
):
    length, cols = q_ref.shape
    heads = b_ref.shape[1]
    part = qv0_ref.shape[0]
    core = core_ref[0]
    block = nm_ref.shape[0] // 2
    for src, side in ((nm_ref, core), (np_ref, 1 - core)):
        qv = mul(src[:, :part], qv0_ref[...]) + mul(src[:, part:], qv1_ref[...])
        for n in range(2):
            there = pl.ds(pl.multiple_of((2 * n + side) * block, block), block)
            here = slice(n * block, (n + 1) * block)
            q_ref[there, :] = qv[here, :cols].astype(BF)
            v_ref[there, :] = qv[here, cols:].astype(BF)
    dim = cols // heads
    half = length // 2
    soft = dim ** -0.5
    row, col = grid_of(length, half, 0, 0)
    row1, col1 = grid_of(half, half, half, half)
    begin = first_of(lax.broadcasted_iota(jnp.int32, (length, 1), 0), starts_ref)
    from_doc = col >= begin
    upto_a = from_doc & (col <= row)
    upto_b = (col1 >= begin[half:]) & (col1 <= row1)
    for h in range(heads):
        at = slice(h * dim, (h + 1) * dim)
        _, wdir, beta = directions(u_ref[:, at], b_ref[:, h : h + 1])
        wb = (wdir * beta).astype(BF)
        q, k, v = q_ref[:, at], k_ref[:, at], v_ref[:, at]
        c00, c1 = c_ref[h, :half, :half], c_ref[h, half:, :]
        xa = jnp.where(upto_a, mul_t(q, wb[:half]), 0.0).astype(BF)
        xb = jnp.where(upto_b, mul_t(q[half:], wb[half:]), 0.0).astype(BF)
        sa = mul_t(q, k[:half]) - mul(xa, c00)
        s0 = jnp.where(upto_a[:half], sa[:half], -1e30)
        low = mul(xb, c1)
        s10 = jnp.where(from_doc[half:], sa[half:] - low[:, :half], -1e30)
        s11 = jnp.where(upto_b, mul_t(q[half:], k[half:]) - low[:, half:], -1e30)
        top = jnp.max(s0, -1, keepdims=True)
        w = jnp.exp((s0 - top) * soft)
        w = (w * (1.0 / jnp.sum(w, -1, keepdims=True))).astype(BF)
        p_ref[h, :half, :half] = w
        o_ref[:half, at] = mul(w, v[:half]).astype(BF)
        s1 = jnp.concatenate([s10, s11], 1)
        top = jnp.max(s1, -1, keepdims=True)
        w = jnp.exp((s1 - top) * soft)
        w = (w * (1.0 / jnp.sum(w, -1, keepdims=True))).astype(BF)
        p_ref[h, half:, :] = w
        o_ref[half:, at] = mul(w, v).astype(BF)
    for n in range(2):
        here = slice(n * block, (n + 1) * block)
        for dst, side in ((send_ref, 1 - core), (keep_ref, core)):
            o = o_ref[pl.ds(pl.multiple_of((2 * n + side) * block, block), block), :]
            dst[here, :part] = mul(o, wo0_ref[...]).astype(dst.dtype)
            dst[here, part:] = mul(o, wo1_ref[...]).astype(dst.dtype)


def backward_kernel(
    starts_ref,
    core_ref,
    k_ref,
    u_ref,
    b_ref,
    c_ref,
    t_ref,
    q_ref,
    v_ref,
    p_ref,
    dm_ref,
    dp_ref,
    wo0_ref,
    wo1_ref,
    wu0_ref,
    wu1_ref,
    wk0_ref,
    wk1_ref,
    qv0_ref,
    qv1_ref,
    nm_ref,
    np_ref,
    duk_out,
    dqv_out,
    keep_ref,
    send_ref,
    gain_ref,
    do_ref,
    duk_ref,
    dqv_ref,
):
    part = wu0_ref.shape[0]
    wide = duk_ref.shape[1]
    near = wu0_ref.shape[1]
    core = core_ref[0]
    block = dm_ref.shape[0] // 2
    for src, side in ((dm_ref, core), (dp_ref, 1 - core)):
        d = mul_t(src[:, :part], wo0_ref[...]) + mul_t(src[:, part:], wo1_ref[...])
        for n in range(2):
            there = pl.ds(pl.multiple_of((2 * n + side) * block, block), block)
            do_ref[there, :] = d[n * block : (n + 1) * block].astype(BF)
    length = q_ref.shape[0]
    heads = b_ref.shape[1]
    dim = q_ref.shape[1] // heads
    half = length // 2
    soft = dim ** -0.5
    row, col = grid_of(length, half, 0, 0)
    row1, col1 = grid_of(half, half, half, half)
    begin = first_of(lax.broadcasted_iota(jnp.int32, (length, 1), 0), starts_ref)
    from_doc = col >= begin
    strict_a = from_doc & (col < row)
    upto_a = from_doc & (col <= row)
    strict_b = (col1 >= begin[half:]) & (col1 < row1)
    upto_b = (col1 >= begin[half:]) & (col1 <= row1)
    early, late = grid_of(half, length, 0, 0)
    begin_t = first_of(lax.broadcasted_iota(jnp.int32, (1, length), 1), starts_ref)
    from_doc_t = early >= begin_t
    upto_a_t = from_doc_t & (early <= late)
    early1, late1 = grid_of(half, half, half, half)
    upto_b_t = (early1 >= begin_t[:, half:]) & (early1 <= late1)
    dbraws = []
    for h in range(heads):
        at = slice(h * dim, (h + 1) * dim)
        scale, wdir, beta = directions(u_ref[:, at], b_ref[:, h : h + 1])
        wd, wb = wdir.astype(BF), (wdir * beta).astype(BF)
        q, k, v, do = q_ref[:, at], k_ref[:, at], v_ref[:, at], do_ref[:, at]
        qt, wdt, dot_ = q.T, wd.T, do.T
        p0, p1 = p_ref[h, :half, :half], p_ref[h, half:, :]
        c00, c1 = c_ref[h, :half, :half], c_ref[h, half:, :]
        t0, t1 = t_ref[h, 0], t_ref[h, 1]
        p0f, p1f = p0.astype(F32), p1.astype(F32)
        dp0 = mul_t(do[:half], v[:half])
        dp1 = mul_t(do[half:], v)
        ds0 = p0f * (dp0 - jnp.sum(p0f * dp0, -1, keepdims=True)) * soft
        ds1 = p1f * (dp1 - jnp.sum(p1f * dp1, -1, keepdims=True)) * soft
        ds0, ds1 = ds0.astype(BF), ds1.astype(BF)
        dsa = jnp.concatenate([ds0, ds1[:, :half]], 0)
        dxa = jnp.where(upto_a, mul_t(dsa, c00), 0.0).astype(BF)
        dxb = jnp.where(upto_b, mul_t(ds1, c1), 0.0).astype(BF)
        xta = jnp.where(upto_a_t, mul_t(wb[:half], q), 0.0).astype(BF)
        xtb = jnp.where(upto_b_t, mul_t(wb[half:], q[half:]), 0.0).astype(BF)
        lta = jnp.where(from_doc_t[:, half:], mul_t(wb[:half], wd[half:]), 0.0).astype(BF)
        dc00 = mul(xta, dsa)
        dc1 = mul(xtb, ds1).astype(BF)
        z1 = mul(t1, dc1)
        z10 = jnp.where(from_doc[half:], z1[:, :half], 0.0).astype(BF)
        z11 = jnp.where(strict_b, z1[:, half:], 0.0).astype(BF)
        z00 = mul(t0, (dc00 - mul(lta, z10)).astype(BF))
        z00 = jnp.where(strict_a[:half], z00, 0.0).astype(BF)
        za = jnp.concatenate([z00, z10], 0)
        z1 = jnp.concatenate([z10, z11], 1)
        dla = jnp.where(strict_a, mul_t(za, c00), 0.0).astype(BF)
        dlb = jnp.where(strict_b, mul_t(z1, c1), 0.0).astype(BF)
        dq0 = mul(ds0, k[:half]) - mul(dxa[:half], wb[:half])
        dq1 = mul(ds1, k) - mul(dxa[half:], wb[:half]) - mul(dxb, wb[half:])
        dk0 = mul(qt, dsa) - mul(wdt, za)
        dk1 = mul(qt[:, half:], ds1[:, half:]) - mul(wdt[:, half:], z11)
        y0 = mul(wdt, dla) - mul(qt, dxa)
        y1 = mul(wdt[:, half:], dlb) - mul(qt[:, half:], dxb)
        dv0 = mul(dot_[:, :half], p0) + mul(dot_[:, half:], p1[:, :half])
        dv1 = mul(dot_[:, half:], p1[:, half:])
        dw0 = mul(dla[:half], wb[:half]) - mul(z00, k[:half])
        dw1 = mul(dla[half:], wb[:half]) + mul(dlb, wb[half:]) - mul(z1, k)
        y = jnp.concatenate([y0, y1], 1).T
        dwd = beta * y + jnp.concatenate([dw0, dw1], 0)
        dbeta = jnp.sum(wdir * y, -1, keepdims=True)
        du = scale * (dwd - wdir * jnp.sum(wdir * dwd, -1, keepdims=True))
        dqv_ref[:half, at] = dq0.astype(BF)
        dqv_ref[half:, at] = dq1.astype(BF)
        dqv_ref[:, (heads + h) * dim : (heads + h + 1) * dim] = (
            jnp.concatenate([dv0, dv1], 1).T.astype(BF)
        )
        duk_ref[:, at] = du.astype(BF)
        behind = wide - heads * dim
        duk_ref[:, behind + h * dim : behind + (h + 1) * dim] = (
            jnp.concatenate([dk0, dk1], 1).T.astype(BF)
        )
        dbraws.append(dbeta * beta * (1.0 - 0.5 * beta))
    lane = lax.broadcasted_iota(jnp.int32, (length, wide - 2 * heads * dim), 1)
    last = jnp.zeros(lane.shape, F32)
    for h in range(heads):
        last = jnp.where(lane == h, dbraws[h], last)
    duk_ref[:, heads * dim : wide - heads * dim] = last.astype(BF)
    gain = [0.0, 0.0]
    for dst, norm, side, base in (
        (send_ref, np_ref, 1 - core, 2 * block),
        (keep_ref, nm_ref, core, 0),
    ):
        for n in range(2):
            there = pl.ds(pl.multiple_of((2 * n + side) * block, block), block)
            here = slice(base + n * block, base + (n + 1) * block)
            duk, dqv = duk_ref[there, :], dqv_ref[there, :]
            duk_out[here, :] = duk
            dqv_out[here, :] = dqv
            rows = slice(n * block, (n + 1) * block)
            du, dk = duk[:, :near], duk[:, near:]
            for i, (cut, wu, wk, qv) in enumerate(
                (
                    (slice(0, part), wu0_ref, wk0_ref, qv0_ref),
                    (slice(part, 2 * part), wu1_ref, wk1_ref, qv1_ref),
                )
            ):
                dn = mul_t(du, wu[...]) + mul_t(dk, wk[...]) + mul_t(dqv, qv[...])
                dst[rows, cut] = dn.astype(dst.dtype)
                gain[i] += jnp.sum(dn * norm[rows, cut].astype(F32), 0, keepdims=True)
    gain_ref[:, :part] = gain[0]
    gain_ref[:, part:] = gain[1]


def vmem(n):
    return [pl.BlockSpec(memory_space=pltpu.VMEM)] * n


def smem(n):
    return [pl.BlockSpec(memory_space=pltpu.SMEM)] * n


def shape_of(*dims, kind=BF):
    return jax.ShapeDtypeStruct(dims, kind)


def params(mib=48):
    return pltpu.CompilerParams(vmem_limit_bytes=mib * 2**20)


def cost(us):
    return pl.CostEstimate(flops=int(us * 3e8), bytes_accessed=1000, transcendentals=0)


def attn_solve(starts, core, nm, np_, wu0, wu1, wk0, wk1, bias):
    length, heads = 2 * nm.shape[0], bias.shape[1]
    cols = wk0.shape[1]
    half = length // 2
    return pl.pallas_call(
        solve_kernel,
        in_specs=smem(2) + vmem(7),
        out_specs=vmem(5),
        out_shape=[
            shape_of(length, cols),
            shape_of(length, cols, kind=F32),
            shape_of(length, heads, kind=F32),
            shape_of(heads, length, length),
            shape_of(heads, 2, half, half),
        ],
        compiler_params=params(),
        cost_estimate=cost(12),
        name="attn_solve",
    )(starts, core, nm, np_, wu0, wu1, wk0, wk1, bias)


def attn_forward(starts, core, nm, np_, qv0, qv1, wo0, wo1, k, u, braw, c):
    length, cols = k.shape
    half, width, heads = length // 2, nm.shape[1], braw.shape[1]
    return pl.pallas_call(
        forward_kernel,
        in_specs=smem(2) + vmem(10),
        out_specs=vmem(6),
        out_shape=[
            shape_of(length, cols),
            shape_of(length, cols),
            shape_of(length, cols),
            shape_of(heads, length, length),
            shape_of(half, width, kind=F32),
            shape_of(half, width),
        ],
        compiler_params=params(),
        cost_estimate=cost(9),
        name="attn_forward",
    )(starts, core, nm, np_, qv0, qv1, wo0, wo1, k, u, braw, c)


def attn_backward(starts, core, saved, dm, dp, *weights_and_norms):
    length, cols = saved[0].shape
    half, width = length // 2, dm.shape[1]
    near, far = weights_and_norms[2].shape[1], weights_and_norms[4].shape[1]
    return pl.pallas_call(
        backward_kernel,
        in_specs=smem(2) + vmem(20),
        out_specs=vmem(5),
        out_shape=[
            shape_of(length, near + far),
            shape_of(length, 2 * cols),
            shape_of(half, width, kind=F32),
            shape_of(half, width),
            shape_of(1, width, kind=F32),
        ],
        scratch_shapes=[
            pltpu.VMEM((length, cols), BF),
            pltpu.VMEM((length, near + far), BF),
            pltpu.VMEM((length, 2 * cols), BF),
        ],
        compiler_params=params(),
        cost_estimate=cost(21),
        name="attn_backward",
    )(starts, core, *saved, dm, dp, *weights_and_norms)


def feed_kernel(a_ref, w0_ref, w1_ref, keep_ref, send_ref):
    rows = a_ref.shape[0] // 2
    part = w0_ref.shape[1]
    for dst, at in ((send_ref, slice(rows, None)), (keep_ref, slice(0, rows))):
        dst[0, :, :part] = mul(a_ref[at, :], w0_ref[...]).astype(dst.dtype)
        dst[0, :, part:] = mul(a_ref[at, :], w1_ref[...]).astype(dst.dtype)


def ffn_feed(act, wd0, wd1):
    hidden, part = wd0.shape
    micros, rows = 2, act.shape[0] // 4
    weight = pl.BlockSpec((hidden, part), lambda m: (0, 0))
    out = pl.BlockSpec((1, rows, 2 * part), lambda m: (m, 0, 0))
    return pl.pallas_call(
        feed_kernel,
        grid=(micros,),
        in_specs=[pl.BlockSpec((2 * rows, hidden), lambda m: (m, 0)), weight, weight],
        out_specs=[out, out],
        out_shape=[
            shape_of(micros, rows, 2 * part, kind=F32),
            shape_of(micros, rows, 2 * part),
        ],
        compiler_params=params(),
        cost_estimate=cost(6),
        name="ffn_feed",
    )(act, wd0, wd1)


def ffn_grad_kernel(*refs):
    a, b = refs[:4], refs[4:6]
    own_ref, far_ref, turned = refs[6:]
    rows = a[0].shape[0]
    part = own_ref.shape[0]

    @pl.when(pl.program_id(0) == 0)
    def _():
        for p in range(4):
            turned[:, p * rows : (p + 1) * rows] = a[p][...].T

    out = mul(turned[:, : 2 * rows], b[0][...]) + mul(turned[:, 2 * rows :], b[1][...])
    own_ref[...] = out[:part].astype(BF)
    far_ref[...] = out[part:].astype(BF)


def ffn_grad(a, b, tile=256):
    rows, width = a[0].shape
    hidden = b[0].shape[1]
    whole = pl.BlockSpec((rows, width), lambda i: (0, 0))
    cols = pl.BlockSpec((2 * rows, tile), lambda i: (0, i))
    out = pl.BlockSpec((width // 2, tile), lambda i: (0, i))
    return pl.pallas_call(
        ffn_grad_kernel,
        grid=(hidden // tile,),
        in_specs=[whole] * 4 + [cols] * 2,
        out_specs=[out, out],
        out_shape=[shape_of(width // 2, hidden)] * 2,
        scratch_shapes=[pltpu.VMEM((width, 4 * rows), BF)],
        compiler_params=params(),
        cost_estimate=cost(6),
        name="ffn_grad",
    )(*a, *b)


def attn_grad_kernel(core_ref, *refs):
    a, d, dqv, duk, attn = refs[:4], refs[4:8], refs[8:10], refs[10:12], refs[12:14]
    extra, own, far = refs[14:16], refs[16:18], refs[18:20]
    turned, turned_d, placed = refs[20:]
    rows = a[0].shape[0]
    block = rows // 2
    part = own[0].shape[0]
    cols = attn[0].shape[1]
    for p in range(4):
        here = slice(p * rows, (p + 1) * rows)
        turned[:, here] = a[p][...].T
        turned_d[:, here] = d[p][...].T
        side = core_ref[0] if p % 2 == 0 else 1 - core_ref[0]
        for n in range(2):
            there = pl.ds(pl.multiple_of((2 * n + side) * block, block), block)
            placed[p * rows + n * block : p * rows + (n + 1) * block, :] = attn[p // 2][there, :]
    ends = [0]
    for o in own:
        ends.append(ends[-1] + o.shape[1])
    pieces = [(cols, cols, 128, duk, 0)]
    at = cols + 128
    for src, begin, size in ((dqv, 0, 2 * cols), (duk, cols + 128, cols), (duk, 0, cols)):
        while size:
            i = max(n for n in range(len(own)) if ends[n] <= at)
            n = min(size, ends[i + 1] - at)
            pieces.append((at - ends[i], begin, n, src, i))
            at, begin, size = at + n, begin + n, size - n
    for side, dsts in ((1, far), (0, own)):
        half = slice(side * part, (side + 1) * part)
        dsts[0][:, :cols] = mul(turned_d[half, :], placed[...]).astype(dsts[0].dtype)
        for to, begin, n, src, i in pieces:
            out = mul(turned[half, : 2 * rows], src[0][:, begin : begin + n])
            out = out + mul(turned[half, 2 * rows :], src[1][:, begin : begin + n])
            if i == 0 and to == cols:
                out = out + extra[side][...]
            dsts[i][:, to : to + n] = out.astype(dsts[i].dtype)


def attn_grad(core, a, d, dqv, duk, attn, extra):
    rows, width = a[0].shape
    part, cols = width // 2, attn[0].shape[1]
    wide = cols + 128
    sizes = (2 * wide,) * 2
    out = pl.pallas_call(
        attn_grad_kernel,
        in_specs=smem(1) + vmem(16),
        out_specs=vmem(4),
        out_shape=[shape_of(part, n) for n in sizes * 2],
        scratch_shapes=[
            pltpu.VMEM((width, 4 * rows), BF),
            pltpu.VMEM((width, 4 * rows), BF),
            pltpu.VMEM((4 * rows, cols), BF),
        ],
        compiler_params=params(),
        cost_estimate=cost(14),
        name="attn_grad",
    )(core, *a, *d, *dqv, *duk, *attn, *extra)
    return list(zip(out[:2], out[2:]))


def up_kernel(*refs):
    n2, g = refs[:4], refs[4:8]
    wg0, wg1, wu0, wu1, one_ref, two_ref, act_ref, own_ref, far_ref = refs[8:]
    part = wg0.shape[0]
    rows = n2[0].shape[0]
    total = 0.0
    for p in range(4):
        a0, a1 = n2[p][:, :part], n2[p][:, part:]
        gate = mul(a0, wg0[...]) + mul(a1, wg1[...])
        upper = mul(a0, wu0[...]) + mul(a1, wu1[...])
        sigma = jax.nn.sigmoid(gate)
        swish = gate * sigma
        act = (swish * upper).astype(BF)
        at = slice(p * rows, (p + 1) * rows)
        one_ref[at, :] = (upper * sigma * (1.0 + gate * (1.0 - sigma))).astype(BF)
        two_ref[at, :] = swish.astype(BF)
        act_ref[at, :] = act
        total = total + mul(act.T, g[p][...])
    own_ref[...] = total[:, :part].astype(BF)
    far_ref[...] = total[:, part:].astype(BF)


def ffn_up(n2, g, wg0, wg1, wu0, wu1, tile=256):
    rows, width = n2[0].shape
    part, hidden = wg0.shape
    whole = pl.BlockSpec((rows, width), lambda i: (0, 0))
    cols = pl.BlockSpec((part, tile), lambda i: (0, i))
    tall = pl.BlockSpec((4 * rows, tile), lambda i: (0, i))
    flat = pl.BlockSpec((tile, part), lambda i: (i, 0))
    return pl.pallas_call(
        up_kernel,
        grid=(hidden // tile,),
        in_specs=[whole] * 8 + [cols] * 4,
        out_specs=[tall] * 3 + [flat] * 2,
        out_shape=[shape_of(4 * rows, hidden)] * 3
        + [shape_of(hidden, part)] * 2,
        compiler_params=params(),
        cost_estimate=cost(16),
        name="ffn_up",
    )(*n2, *g, wg0, wg1, wu0, wu1)


def down_kernel(*refs):
    g, one_ref, two_ref = refs[:2], refs[2], refs[3]
    wd0, wd1, wg0, wg1, wu0, wu1, dg_ref, du_ref, keep_ref, send_ref, acc = refs[4:]
    part = wg0.shape[0]
    rows = g[0].shape[0]
    step = pl.program_id(0)

    for p in range(2):
        d = mul_t(g[p][:, :part], wd0[...]) + mul_t(g[p][:, part:], wd1[...])
        at = slice(p * rows, (p + 1) * rows)
        dg = (d * one_ref[at, :].astype(F32)).astype(BF)
        du = (d * two_ref[at, :].astype(F32)).astype(BF)
        dg_ref[at, :] = dg
        du_ref[at, :] = du
        new0 = mul_t(dg, wg0[...]) + mul_t(du, wu0[...])
        new1 = mul_t(dg, wg1[...]) + mul_t(du, wu1[...])

        @pl.when(step == 0)
        def _():
            acc[at, :part] = new0
            acc[at, part:] = new1

        @pl.when(step > 0)
        def _():
            acc[at, :part] += new0
            acc[at, part:] += new1

    @pl.when(step == pl.num_programs(0) - 1)
    def _():
        keep_ref[...] = acc[:rows, :]
        send_ref[...] = acc[rows:, :].astype(BF)


def ffn_down(m, g, one, two, wd0, wd1, wg0, wg1, wu0, wu1, tile=256):
    rows, width = g[0].shape
    part, hidden = wg0.shape
    whole = pl.BlockSpec((rows, width), lambda i: (0, 0))
    cols = pl.BlockSpec((part, tile), lambda i: (0, i))
    flat = pl.BlockSpec((tile, part), lambda i: (i, 0))
    pick_m = pl.BlockSpec((2 * rows, tile), lambda i: (m, i))
    tall = pl.BlockSpec((2 * rows, tile), lambda i: (0, i))
    return pl.pallas_call(
        down_kernel,
        grid=(hidden // tile,),
        in_specs=[whole] * 2 + [pick_m] * 2 + [flat] * 2 + [cols] * 4,
        out_specs=[tall] * 2 + [whole] * 2,
        out_shape=[shape_of(2 * rows, hidden)] * 2
        + [shape_of(rows, width, kind=F32), shape_of(rows, width)],
        scratch_shapes=[pltpu.VMEM((2 * rows, width), F32)],
        compiler_params=params(),
        cost_estimate=cost(13),
        name="ffn_down",
    )(*g, one, two, wd0, wd1, wg0, wg1, wu0, wu1)


def swap_wid(a):
    return lax.ppermute(a, "wid", [(0, 1), (1, 0)])


def swap_core(a):
    return lax.ppermute(a, "hid", [(0, 1), (1, 0), (2, 3), (3, 2)])


def swap_chip(a):
    return lax.ppermute(a, "hid", [(0, 2), (2, 0), (1, 3), (3, 1)])


def tie(a, *others):
    return lax.optimization_barrier((a, *others))[0]


class RowSum:
    def __init__(self, a):
        self.value = a
        self.line = lax.axis_size("rows") == 4
        self.stage = 0

    def send(self):
        self.stage += 1
        if self.line and self.stage <= 3:
            moves = {1: [(0, 1), (3, 2)], 2: [(1, 2), (2, 1)], 3: [(1, 0), (2, 3)]}
            self.got = lax.ppermute(self.value, "rows", moves[self.stage])

    def take(self, then):
        if not self.line:
            if self.stage == 3:
                self.value = lax.psum(then(self.value), "rows").astype(F32)
        elif self.stage < 3:
            self.value = (self.value.astype(F32) + then(self.got).astype(F32)).astype(BF)
        else:
            place = lax.axis_index("rows")
            inner = (place == 1) | (place == 2)
            self.value = jnp.where(inner, self.value, then(self.got)).astype(F32)


def pick(pair, first):
    a, b = pair
    return jnp.where(first, a, b), jnp.where(first, b, a)

ORDER = (
    "fd0", "low0", "fd1", "low1", "gF", "dL", "dmid0", "ab0", "gL", "dM",
    "dmid1", "uF", "ab1", "dW", "gM", "aF", "uL", "vL", "aL", "bL",
    "uM", "gW", "dE", "vM", "feed", "cL", "eL", "aM", "uW", "gE",
    "bM", "vW", "uE", "flow", "cM", "vE", "aW", "eM", "dlow", "bW",
    "aE", "outs", "cW", "bE", "dxs", "eW", "s1", "cE", "s2", "outsf",
    "s3", "dxsf", "eE",
)


def on_device(
    inputs,
    starts,
    norm_one,
    w_query,
    w_key,
    w_value,
    w_house,
    strength_weight,
    b_beta,
    w_out,
    norm_two,
    gate_weight,
    up_weight,
    w_down,
    cotangent,
):
    micros, _, block, part = inputs.shape
    width = 2 * part
    half = 2 * block
    cols = w_query.shape[1]
    heads = strength_weight.shape[1]
    wid = lax.axis_index("wid")
    hid = lax.axis_index("hid")
    core, chip = hid % 2, hid // 2
    chip0, wid0 = chip == 0, wid == 0
    core_arg = core.astype(jnp.int32).reshape(1)

    def take(a, axis, index):
        return lax.dynamic_index_in_dim(a, index, axis, keepdims=False)

    def assisted(w, *before):
        size = w.shape[0] // lax.axis_size("rows")
        share = lax.dynamic_slice_in_dim(w, lax.axis_index("rows") * size, size)
        got = swap_wid(tie(share, *before))
        return lax.all_gather(got, "rows", axis=0, tiled=True), got

    x_far = swap_wid(take(inputs, 1, 1 - wid))
    gains = jnp.stack([norm_one, norm_two])
    gains_far = swap_wid(gains)
    gains = jnp.concatenate([gains, gains_far], 1)
    w_u = jnp.concatenate([w_house, strength_weight, jnp.zeros((part, 128 - heads), BF)], 1)
    w_qv = jnp.concatenate([w_query, w_value], 1)
    u_far = swap_wid(tie(w_u, x_far))
    k_far = swap_wid(tie(w_key, x_far))
    up_far, up_share = assisted(up_weight, u_far)
    down_far, down_share = assisted(w_down, k_far)
    qv_far = swap_wid(tie(w_qv, u_far))
    g_far = swap_wid(tie(take(cotangent, 1, 1 - wid), k_far))
    out_far = swap_wid(tie(w_out, k_far))
    row_starts = take(starts, 1, wid)

    def gather_chip(mine, far):
        mine = jnp.concatenate([mine, far], -1)
        a, b = pick((mine, swap_chip(mine)), chip0)
        return jnp.stack([a, b], 1).reshape(micros, half, width)

    def chip_sum(keep, send):
        return keep + swap_core(send).astype(F32)

    def my_block(a):
        return take(a.reshape(2, block, a.shape[-1]), 0, chip)

    x_half = tie(gather_chip(take(inputs, 1, wid), x_far), u_far).astype(F32)
    scale_one = lax.rsqrt(jnp.mean(x_half * x_half, -1, keepdims=True) + EPS)
    nm_half = (x_half * scale_one * gains[0]).astype(BF)
    nm_half = tie(nm_half, k_far)
    nm_peer = swap_core(nm_half)
    saved, attns, mids, scales, n2_parts = [], [], [], [], []
    uk_w = (w_u, u_far, w_key, k_far)
    for m in range(micros):
        nm = nm_half[m] if m == 0 else tie(nm_half[m], saved[0][0])
        saved.append(attn_solve(row_starts[m], core_arg, nm, nm_peer[m], *uk_w, b_beta[None]))
    g_half = gather_chip(tie(take(cotangent, 1, wid), saved[-1][0]), g_far)
    def finish_mid(m, low, got):
        mid = x_half[m] + low.astype(F32) + got.astype(F32)
        scale_two = lax.rsqrt(jnp.mean(mid * mid, -1, keepdims=True) + EPS)
        n2 = (mid * scale_two * gains[1]).astype(BF)
        n2_parts.extend([n2, swap_core(n2)])
        mids.append(mid)
        scales.append(scale_two)

    low = saved[1][0]
    for m in range(micros):
        k, u, braw, c, t = saved[m]
        nm = tie(nm_half[m], low)
        q, v, attn, p, keep, send = attn_forward(
            row_starts[m], core_arg, nm, nm_peer[m], w_qv, qv_far, w_out, out_far, k, u, braw, c
        )
        saved[m] = (*saved[m], q, v, p)
        attns.append(attn)
        got = swap_core(send)
        if m == 1:
            finish_mid(0, low, tie(chip_got, keep))
            got = tie(got, n2_parts[0])
        low = (keep + got.astype(F32)).astype(BF)
        chip_got = swap_chip(low)
    finish_mid(1, low, chip_got)
    g_peer = swap_core(tie(g_half, low))
    g_parts = [a for m in range(micros) for a in (g_half[m], g_peer[m])]
    gate_far = swap_wid(tie(gate_weight, saved[1][0]))
    ffn_w = (gate_weight, gate_far, up_weight, up_far)
    one, two, act, down_own, down_far_part = ffn_up(n2_parts, g_parts, *ffn_w)
    ready = {"d": (down_own, swap_wid(down_far_part), slice(None))}

    last = [act]

    def then(a):
        return tie(a, last[0])

    def mark(a):
        last[0] = a
        return a

    s = {}
    steps = {}

    def stack_m(name):
        return jnp.concatenate([s[name + "0"], s[name + "1"]], 0)

    def row_steps(m, tag):
        def ffn_back():
            gm = (then(g_parts[2 * m]), g_parts[2 * m + 1])
            dg, du, keep, send = ffn_down(m, gm, one, two, w_down, down_far, *ffn_w)
            s["dg" + tag], s["du" + tag], s["nk" + tag] = mark(dg), du, keep
            s["ng" + tag] = swap_core(send)

        def low():
            s["nl" + tag] = mark((s["nk" + tag] + then(s["ng" + tag]).astype(F32)).astype(BF))
            s["nx" + tag] = swap_chip(s["nl" + tag])

        def d_mid():
            mid, scale = mids[m], scales[m]
            dn = s["nl" + tag].astype(F32) + then(s["nx" + tag]).astype(F32)
            inner = jnp.mean(mid * gains[1] * dn, -1, keepdims=True)
            d = g_half[m].astype(F32) + scale * gains[1] * dn
            d = d - mid * scale * scale * scale * inner
            s["d" + tag] = d
            s["g2" + tag] = 0.5 * jnp.sum(dn * mid * scale, 0)
            s["dl" + tag] = mark(d.astype(BF))
            s["dp" + tag] = swap_core(s["dl" + tag])

        def attn_back():
            duk, dqv, keep, send, s["g1" + tag] = attn_backward(
                row_starts[m],
                core_arg,
                saved[m],
                then(s["dl" + tag]),
                s["dp" + tag],
                w_out,
                out_far,
                *uk_w,
                w_qv,
                qv_far,
                nm_half[m],
                nm_peer[m],
            )
            s["duk" + tag], s["dqv" + tag], s["ak" + tag] = mark(duk), dqv, keep
            s["ag" + tag] = swap_core(send)

        steps["fd" + tag] = ffn_back
        steps["low" + tag] = low
        steps["dmid" + tag] = d_mid
        steps["ab" + tag] = attn_back

    for m in range(micros):
        row_steps(m, str(m))

    def grad_steps(name):
        state = {}

        def low():
            own, near, part_of = ready[name]
            near = then(near)[:, part_of].astype(F32)
            state["sum"] = RowSum(mark((own[:, part_of].astype(F32) + near).astype(BF)))
            state["sum"].send()

        def more():
            state["sum"].take(then)
            mark(state["sum"].value)
            state["sum"].send()

        def end():
            more()
            s[name] = state["sum"].value

        steps[name + "L"] = low
        steps[name + "M"] = more
        steps[name + "W"] = more
        steps[name + "E"] = end

    for name in "dguvabce":
        grad_steps(name)

    def put_ready(names, own, near):
        size = own.shape[1] // len(names)
        for n, name in enumerate(names):
            ready[name] = (own, near, slice(n * size, (n + 1) * size))

    def ffn_grad_step(name, of):
        def step():
            norms = (then(n2_parts[0]), *n2_parts[1:])
            b = (s[of + "0"], s[of + "1"])
            own, far = ffn_grad(norms, b)
            put_ready(name, own, swap_wid(mark(far)))

        return step

    steps["gF"] = ffn_grad_step("g", "dg")
    steps["uF"] = ffn_grad_step("uv", "du")

    def feed_step():
        keep, send = ffn_feed(then(act), w_down, down_far)
        mark(keep)
        for m in range(micros):
            s[f"fk{m}"], s[f"fg{m}"] = keep[m], swap_core(send[m])

    steps["feed"] = feed_step

    def attn_grad_step():
        duk = [s["duk0"], s["duk1"]]
        bias = sum(jnp.sum(a[:, cols : cols + heads].astype(F32), 0) for a in duk)
        scales = jnp.stack([(s["g10"] + s["g11"])[0] / gains[0], s["g20"] + s["g21"]], 1)
        column = lax.broadcasted_iota(jnp.int32, (width, 128), 1)
        row = lax.broadcasted_iota(jnp.int32, (width, 128), 0) % part
        extra = jnp.where(column == 2 * heads, scales[:, :1], 0.0)
        extra = extra + jnp.where(column == 2 * heads + 1, scales[:, 1:], 0.0)
        bias = jnp.pad(bias[None], ((0, 0), (heads, 128 - 2 * heads)))
        extra = extra + jnp.where(row == 0, bias, 0.0)
        norms = [a for m in range(micros) for a in (nm_half[m], nm_peer[m])]
        norms[0] = then(norms[0])
        dqv = [s["dqv0"], s["dqv1"]]
        db = [s["dl0"], s["dp0"], s["dl1"], s["dp1"]]
        pairs = attn_grad(core_arg, norms, db, dqv, duk, attns, (extra[:part], extra[part:]))
        mark(pairs[0][1])
        for names, (own, far) in zip(("ab", "ce"), pairs):
            put_ready(names, own, swap_wid(far))

    steps["aF"] = attn_grad_step

    def own_blocks(a):
        return jnp.stack([my_block(m) for m in a])

    def block_low(keep, got, name):
        def step():
            low = [s[keep + t] + then(s[got + t]).astype(F32) for t in ("0", "1")]
            low = jnp.stack(low).reshape(micros, 2, block, width)
            s[name + "l"] = take(low, 1, chip)
            s[name + "x"] = swap_chip(mark(take(low, 1, 1 - chip).astype(BF)))

        return step

    def rows_back(values, kind, name):
        own = values[..., :part].astype(kind)
        far = swap_wid(mark(values[..., part:].astype(BF)))

        def finish():
            a, b = pick((own, then(far).astype(kind)), wid0)
            s[name] = mark(jnp.stack([a, b], 1))

        steps[name + "f"] = finish

    def out_step():
        rows_back(own_blocks(mids) + s["fl"] + then(s["fx"]).astype(F32), BF, "outs")

    def dx_step():
        dn = s["al"] + then(s["ax"]).astype(F32)
        x, scale = own_blocks(x_half), own_blocks(scale_one)
        inner = jnp.mean(x * gains[0] * dn, -1, keepdims=True)
        dx = own_blocks([s["d0"], s["d1"]]) + scale * gains[0] * dn
        rows_back(dx - x * scale * scale * scale * inner, F32, "dxs")

    def small_core():
        s["few"] = then(s["a"])[:, cols + 2 * heads : cols + 2 * heads + 2]
        s["few_got"] = swap_core(s["few"])

    def small_chip():
        s["few"] = mark(s["few"] + then(s["few_got"]))
        s["few_got"] = swap_chip(s["few"])

    def small_end():
        s["small"] = mark(s["few"] + then(s["few_got"]))

    steps["s1"], steps["s2"], steps["s3"] = small_core, small_chip, small_end
    steps["flow"] = block_low("fk", "fg", "f")
    steps["dlow"] = block_low("ak", "ag", "a")
    steps["outs"] = out_step
    steps["dxs"] = dx_step
    for name in ORDER:
        steps[name]()
    outs, dxs = s["outs"], s["dxs"]
    g_down, g_gate, g_up = s["d"], s["g"], jnp.concatenate([s["u"], s["v"]], 1)
    g_out = s["a"][:, :cols].T
    strengths = s["a"][:, cols:]
    chunks = (s["b"], s["c"], s["e"])
    wide = cols + 128

    def columns(begin):
        out = []
        done = 0
        while done < cols:
            at = begin + done
            n = min(cols - done, wide - at % wide)
            out.append(chunks[at // wide][:, at % wide : at % wide + n])
            done += n
        return jnp.concatenate(out, 1)

    g_q, g_v, g_k, g_u = [columns(n * cols) for n in range(4)]
    return (
        outs,
        dxs,
        s["small"][:, 0],
        g_q,
        g_k,
        g_v,
        g_u,
        strengths[:, :heads],
        strengths[0, heads : 2 * heads],
        g_out,
        s["small"][:, 1],
        g_gate,
        g_up,
        g_down,
    )


def solution(mesh):
    tokens = P(None, "rows", "hid", "wid")
    tall, flat = P("wid", "hid"), P("hid", "wid")
    specs = (P("wid"), tall, tall, tall, tall, tall, P("hid"), flat, P("wid"), tall, tall, flat)
    return jax.shard_map(
        on_device,
        mesh=mesh,
        in_specs=(tokens, P(None, "rows", None), *specs, tokens),
        out_specs=(tokens, tokens, *specs),
        check_vma=False,
    )
```
